512 devices in a mesh: grp: 4 (over x), dp: 16 (over y, core), tensor: 8 (over z).
Axes of the slice: x: 4, y: 8, z: 8, core: 2. Of those that a mesh axis runs over, the one named last changes fastest.
Arguments:
- queries: bfloat16 [512, 64, 576], P(('grp', 'dp'), 'tensor'), may hold values from -1006 to 1006
- latent_cache: bfloat16 [512, 128, 576], P(('grp', 'dp')), may hold values from -4 to 4
- lengths: int32 [512], P(('grp', 'dp')), may hold values from 2 to 128, as said below
- value_up: bfloat16 [64, 512, 128], P('tensor'), may hold values from -0.25 to 0.25
- out_proj: bfloat16 [8192, 7168], P('tensor', 'dp'), may hold values from -0.1875 to 0.1875
- residual_in: bfloat16 [512, 7168], P(('grp', 'tensor'), 'dp'), may hold values from -12 to 12
- norm_gain: bfloat16 [7168], P('dp'), may hold values from 0.099609375 to 1.8984375
- router: bfloat16 [16, 7168], P('grp', 'dp'), may hold values from -0.0625 to 0.0625
- gate_up: bfloat16 [16, 7168, 2, 1024], P('grp', 'dp', None, 'tensor'), may hold values from -0.0625 to 0.0625
- down_proj: bfloat16 [16, 1024, 7168], P('grp', 'tensor', 'dp'), may hold values from -0.5 to 0.5
- routes: int32 [512, 8], P(('grp', 'tensor')), may hold values from 0 to 15, all different within a row; in each aligned block of 16 rows (0 to 15, 16 to 31, ...) at most 12 rows name the same one
- expert_slot: int32 [16], replicated, may hold values from 0 to 15, each once
Outputs:
- layer_out: bfloat16 [512, 7168], P(('grp', 'tensor'), 'dp')
The draws below stay inside these ranges and needn't reach their ends.
Inputs may be any that keep to these rules, and one draw needn't show every extreme that they name: `routes`: each row names 8 different experts; within each aligned block of 16 rows (the rows of one device) no expert is named by more than 12 rows, and some block reaches it. `expert_slot`: a permutation. `lengths`: some sequence uses all 128 positions.
All inputs are finite; a program needn't handle non-finite values.
Results may differ from the reference program's by a relative error of at most 0.012.
Values may be sent and summed in bfloat16 or wider, within the bound.
A program may use at most 64 MiB of HBM per device.

```python
import math
import jax
import jax.numpy as jnp
import numpy as np
from jax import lax

D = 7168
FFE = 1024
HEADS = 64
LAT = 512
ROPE = 64
VHEAD = 128
TOP = 8
CACHE = 128
SEQS = 512
EXPERTS = 16
R_DEV = 16
CAP = 12


def cache_base(key):
    values = jax.random.normal(key, (SEQS, CACHE, LAT + ROPE), jnp.float32)
    return jnp.clip(values, -4.0, 4.0)


def draw_latent_cache(key, part):
    stored = cache_base(key)
    return stored.astype(jnp.bfloat16)


def draw_queries(key, part):
    key = jax.random.fold_in(key, 7)
    values = jnp.clip(jax.random.normal(key, (SEQS, HEADS, LAT + ROPE), jnp.float32), -4.0, 4.0)
    return values.astype(jnp.bfloat16)


def draw_lengths(key, part):
    key = jax.random.fold_in(key, 3)
    drawn_len = jax.random.randint(key, (SEQS,), 2, CACHE + 1)
    chosen_seq = jax.random.randint(jax.random.fold_in(key, 1), (), 0, SEQS)
    return drawn_len.at[chosen_seq].set(CACHE).astype(jnp.int32)


def draw_residual_in(key, part):
    key = jax.random.fold_in(key, 9)
    row_key = jax.random.fold_in(key, 1)
    column = lax.broadcasted_iota(jnp.float32, (1, D), 1) / D
    row_scale = jnp.exp(jax.random.uniform(row_key, (SEQS, 1), jnp.float32, jnp.log(0.2), jnp.log(2.0)))
    column_scale = 0.2 * 10.0 ** column
    noise = jnp.clip(jax.random.normal(key, (SEQS, D), jnp.float32), -3.0, 3.0)
    return (noise * row_scale * column_scale).astype(jnp.bfloat16)


def steps_of(key, shape, shards, least, largest):
    def one(dim, shards_of):
        draws = jax.random.uniform(jax.random.fold_in(jax.random.fold_in(key, 6), dim), (shards_of,), jnp.float32, least / len(shards), largest / len(shards))
        return jnp.repeat(jnp.exp(draws), shape[dim] // shards_of).reshape((-1,) + (1,) * (len(shape) - dim - 1))

    gain = one(*shards[0])
    for cut in shards[1:]:
        gain = gain * one(*cut)
    return gain


def routed_block(own_key, own, number, rows, count, top, reach, skew):
    sequence = jax.random.permutation(own_key, count)
    heavy_load, usual = portions_of(count, rows * top, reach, skew, True), portions_of(count, rows * top, reach, skew, False)
    places = jnp.arange(count)

    def named(tallies, turn):
        used = int((tallies > 0).sum())
        fixed = max(1, used // 4)
        passed = fixed + (places - fixed + turn * (used - fixed)) % max(1, count - fixed)
        return jnp.zeros((count,), jnp.int32).at[sequence[jnp.where(places < fixed, places, passed)]].set(jnp.asarray(tallies, jnp.int32))

    tallies = jnp.where(number % 4 == 0, named(heavy_load, number // 4), named(usual, number - number // 4 - 1))
    mixed = jax.random.permutation(jax.random.fold_in(own, 3), count)
    giver, sink = mixed[0:count // 2 * 2:2], mixed[1:count // 2 * 2:2]
    slack = jnp.minimum(tallies[giver] - 1, reach - tallies[sink]) // 2
    slack = jnp.where((giver == sequence[0]) | (sink == sequence[0]) | (tallies[sink] == 0), 0, jnp.maximum(slack, 0))
    passed = jax.random.randint(jax.random.fold_in(own, 4), (count // 2,), 0, 1 << 20) % (slack + 1)
    tallies = tallies.at[giver].add(-passed).at[sink].add(passed)
    items = jnp.searchsorted(jnp.cumsum(tallies), jnp.arange(rows * top), side="right").astype(jnp.int32)
    grid = items.reshape(top, rows).T
    grid = grid[jax.random.permutation(jax.random.fold_in(own, 1), rows)]
    turn = jax.random.randint(jax.random.fold_in(own, 2), (rows, 1), 0, top)
    return jnp.take_along_axis(grid, (jnp.arange(top)[None, :] + turn) % top, axis=1)


def portions_of(amount, total, bound, slope, full):
    weights = [(1 << 20) // math.isqrt(rank ** slope) + 1 for rank in range(1, amount + 1)]
    largest = bound if full else min(bound, max(-(-total // amount), total * weights[0] // sum(weights)))
    least = 1 if total - largest >= amount - 1 else 0
    holding, surplus = [largest] + [least] * (amount - 1), total - largest - least * (amount - 1)
    while surplus > 0:
        free = [i for i in range(1, amount) if holding[i] < largest] or [i for i in range(1, amount) if holding[i] < bound]
        whole, left = sum([weights[i] for i in free]), surplus
        for i in free:
            extra = min(bound - holding[i], max(1, left * weights[i] // whole), surplus)
            holding[i] = holding[i] + extra
            surplus = surplus - extra
    return np.array(holding)


def scatter_about(rng, dims, spread, bound, pieces=(), held_as=jnp.bfloat16):
    drawn = jax.random.normal(rng, dims, jnp.float32) * spread
    if len(pieces) > 0:
        drawn = steps_of(rng, dims, pieces, -0.22, 0.18) * drawn
    return jnp.clip(drawn, min=-bound, max=bound).astype(held_as)


def setup_inputs(seed: int = 0) -> dict:
    splits = jax.random.split(jax.random.key(seed), 13)
    queries = draw_queries(jax.random.fold_in(splits[12], 71), 0)
    latent_cache = draw_latent_cache(jax.random.fold_in(splits[12], 71), 0)
    lengths = draw_lengths(jax.random.fold_in(splits[12], 71), 0)
    value_up = scatter_about(splits[3], (HEADS, LAT, VHEAD), LAT ** -0.5, 0.25, ((0, 8),))
    out_proj = scatter_about(splits[4], (HEADS * VHEAD, D), (HEADS * VHEAD // 8) ** -0.5, 0.1875, ((0, 8), (1, 16)))
    residual_in = draw_residual_in(jax.random.fold_in(splits[12], 71), 0)
    norm_gain = jnp.clip(1.0 + 0.18 * jax.random.normal(splits[6], (D,), jnp.float32), 0.099609375, 1.8984375).astype(jnp.bfloat16)
    router = scatter_about(splits[7], (EXPERTS, D), D ** -0.5, 0.0625, ((0, 4), (1, 16)))
    gate_up = scatter_about(splits[8], (EXPERTS, D, 2, FFE), D ** -0.5, 0.0625, ((0, 4), (1, 16), (3, 8)))
    down_proj = scatter_about(splits[9], (EXPERTS, FFE, D), (FFE // 8) ** -0.5, 0.5, ((0, 4), (1, 8), (2, 16)))
    routes_keys = jax.random.split(jax.random.fold_in(splits[10], 1), SEQS // R_DEV)
    routes_turns = jax.random.permutation(jax.random.fold_in(splits[10], 3), SEQS // R_DEV)
    routes = jax.vmap(lambda own, number: routed_block(jax.random.fold_in(splits[10], 2), own, number, R_DEV, EXPERTS, TOP, CAP, 2))(routes_keys, routes_turns).reshape((SEQS, TOP))
    expert_slot = jax.random.permutation(splits[11], EXPERTS).astype(jnp.int32)
    return {"queries": queries, "latent_cache": latent_cache, "lengths": lengths, "value_up": value_up, "out_proj": out_proj, "residual_in": residual_in, "norm_gain": norm_gain, "router": router, "gate_up": gate_up, "down_proj": down_proj, "routes": routes, "expert_slot": expert_slot}


EPSILON = 1e-06

def attend(queries, latent_cache, lengths, value_up):
    score_scale = (VHEAD + ROPE) ** (-0.5)
    scores = jnp.einsum('nhc,njc->nhj', queries.astype(jnp.float32), latent_cache.astype(jnp.float32)) * score_scale
    positions = jnp.arange(CACHE, dtype=jnp.int32)
    in_cache = positions[None, None, :] < lengths[:, None, None]
    scores = jnp.where(in_cache, scores, -1e+30)
    row_max = lax.optimization_barrier(jnp.max(scores, axis=2, keepdims=True))
    weights = jnp.exp(scores - row_max)
    prob_rows = (weights / lax.optimization_barrier(jnp.sum(weights, axis=2, keepdims=True))).astype(jnp.bfloat16)
    latent = jnp.einsum('nhj,njc->nhc', prob_rows.astype(jnp.float32), latent_cache[:, :, :LAT].astype(jnp.float32)).astype(jnp.bfloat16)
    head_out = jnp.einsum('nhc,hcv->nhv', latent.astype(jnp.float32), value_up.astype(jnp.float32)).astype(jnp.bfloat16)
    return head_out.reshape(head_out.shape[0], HEADS * VHEAD)

def reference(queries, latent_cache, lengths, value_up, out_proj, residual_in, norm_gain, router, gate_up, down_proj, routes, expert_slot):
    head_out = attend(queries, latent_cache, lengths, value_up)
    attn_out = jnp.dot(head_out, out_proj, preferred_element_type=jnp.float32)
    stream = (residual_in.astype(jnp.float32) + attn_out).astype(jnp.bfloat16)
    wide_stream = stream.astype(jnp.float32)
    scaled = (wide_stream * norm_gain.astype(jnp.float32)[None, :]).astype(jnp.bfloat16)
    inv_rms = lax.rsqrt(lax.optimization_barrier(jnp.mean(wide_stream * wide_stream, axis=1)) + EPSILON)
    slot_of = expert_slot[routes]
    slot_range = jnp.arange(EXPERTS, dtype=jnp.int32)
    chosen = lax.optimization_barrier(jnp.sum((slot_of[:, :, None] == slot_range[None, None, :]).astype(jnp.float32), axis=1))

    def one_expert(carry, item):
        numerator, denominator = carry
        weight_gu, weight_down, weight_route, slot_index = item
        gate_up_sum = jnp.dot(scaled, weight_gu.reshape(D, 2 * FFE), preferred_element_type=jnp.float32) * inv_rms[:, None]
        hidden = (jax.nn.silu(gate_up_sum[:, :FFE]) * gate_up_sum[:, FFE:]).astype(jnp.bfloat16)
        expert_out = jnp.dot(hidden, weight_down, preferred_element_type=jnp.float32)
        router_logit = jnp.dot(scaled, weight_route, preferred_element_type=jnp.float32) * inv_rms
        picked = lax.dynamic_index_in_dim(chosen, slot_index, 1, keepdims=False)
        router_score = jax.nn.sigmoid(router_logit) * picked
        return ((numerator + router_score[:, None] * expert_out, denominator + router_score), None)
    start = (jnp.zeros((SEQS, D), jnp.float32), jnp.zeros((SEQS,), jnp.float32))
    (numerator, denominator), unused = lax.scan(one_expert, start, (gate_up, down_proj, router, slot_range))
    moe = numerator / denominator[:, None]
    return (wide_stream + moe).astype(jnp.bfloat16)
```

```python
import functools

import jax
import jax.numpy as jnp
from jax import lax
from jax.experimental import pallas as pl
from jax.experimental.pallas import tpu as pltpu
from jax.sharding import PartitionSpec as P

ROPE = 64
VHEAD = 128
EPSILON = 1e-06
MESH = pl.DeviceIdType.MESH
BF16 = jnp.bfloat16
F32 = jnp.float32
LANES = 128


def dot(a, b):
    return jnp.dot(a, b, preferred_element_type=F32)


def dot_nt(a, b, precision=None):
    return lax.dot_general(
        a, b, (((1,), (1,)), ((), ())), preferred_element_type=F32, precision=precision
    )


def near_first(count):
    return sorted(range(1, count), key=lambda d: (min(d, count - d), d))


def kernel(
    sizes,
    width,
    lengths_ref,
    expert_slot_ref,
    queries_ref,
    residual_ref,
    gain_ref,
    router_ref,
    routes_ref,
    cache_hbm,
    value_up_hbm,
    out_proj_hbm,
    gate_up_hbm,
    down_hbm,
    out_ref,
    cache,
    value_up,
    out_proj,
    gate_up,
    down,
    latent,
    heads,
    proj_out,
    proj_in,
    residual,
    extra,
    stream,
    rows,
    wide,
    weights,
    weights_out,
    router_all,
    router_rows,
    part_out,
    part_in,
    tail_out,
    tail_in,
    hidden,
    down_out,
    down_in,
    sum_out,
    sum_in,
    load_sem,
    head_send,
    head_recv,
    head_core_send,
    head_core_recv,
    weight_send,
    weight_recv,
    router_send,
    router_recv,
    proj_send,
    proj_recv,
    row_z_send,
    row_z_recv,
    row_x_send,
    row_x_recv,
    row_core_send,
    row_core_recv,
    part_send,
    part_recv,
    tail_send,
    tail_recv,
    hid_send,
    hid_recv,
    hid_core_send,
    hid_core_recv,
    down_send,
    down_recv,
    sum_send,
    sum_recv,
):
    nx, ny, nz = sizes
    g = lax.axis_index("grp")
    dp = lax.axis_index("dp")
    t = lax.axis_index("tensor")
    y = dp // 2
    c = lax.rem(dp, 2)
    other = 1 - c
    cols = residual_ref.shape[1]
    block = residual_ref.shape[0]
    wide_cols = stream.shape[1]
    seqs, head_count, depth = queries_ref.shape
    latent_dim = value_up.shape[1]
    local_experts = router_ref.shape[0]
    ys, zs = near_first(ny), near_first(nz)
    xs = near_first(nx)

    def at_x(d):
        return lax.rem(g + nx + d, nx)

    def at_y(d):
        return lax.rem(y + ny + d, ny)

    def at_z(d):
        return lax.rem(t + nz + d, nz)

    def to_x(d):
        return (at_x(d), dp, t)

    def to_y(d):
        return (g, at_y(d) * 2 + c, t)

    def to_z(d):
        return (g, dp, at_z(d))

    partner = (g, y * 2 + other, t)
    sent = []

    def send(src, dst, send_sem, recv_sem, device):
        copy = pltpu.make_async_remote_copy(
            src_ref=src,
            dst_ref=dst,
            send_sem=send_sem,
            recv_sem=recv_sem,
            device_id=device,
            device_id_type=MESH,
        )
        copy.start()
        sent.append(copy)

    def arrived(dst, recv_sem):
        pltpu.make_async_remote_copy(
            src_ref=dst,
            dst_ref=dst,
            send_sem=load_sem.at[0],
            recv_sem=recv_sem,
            device_id=partner,
            device_id_type=MESH,
        ).wait_recv()

    barrier = pltpu.get_barrier_semaphore()
    peers = [partner] + [to_y(d) for d in ys] + [to_z(d) for d in zs] + [to_x(d) for d in xs]
    for device in peers:
        pl.semaphore_signal(barrier, inc=1, device_id=device, device_id_type=MESH)

    loads = [
        pltpu.make_async_copy(src, dst, load_sem.at[i])
        for i, (src, dst) in enumerate(
            [
                (cache_hbm, cache),
                (value_up_hbm, value_up),
                (out_proj_hbm, out_proj),
                (gate_up_hbm, gate_up),
            ]
            + [
                (down_hbm.at[e], down.at[:, pl.ds(e * down_hbm.shape[2], down_hbm.shape[2])])
                for e in range(local_experts)
            ]
        )
    ]
    for load in loads:
        load.start()

    score_scale = (VHEAD + ROPE) ** (-0.5)
    loads[0].wait()
    for n in range(seqs):
        scores = dot(queries_ref[n], cache[n]) * score_scale
        positions = lax.broadcasted_iota(jnp.int32, scores.shape, 1)
        scores = jnp.where(positions < lengths_ref[n], scores, -1e30)
        exps = jnp.exp(scores - jnp.max(scores, axis=1, keepdims=True))
        probs = (exps / jnp.sum(exps, axis=1, keepdims=True)).astype(BF16)
        of_seq = dot_nt(probs, cache[n, :latent_dim, :])
        for q in range(latent_dim // LANES):
            latent[q, n * head_count : (n + 1) * head_count, :] = of_seq[
                :, q * LANES : (q + 1) * LANES
            ]
    loads[1].wait()
    half = head_count // 2
    for low in range(half):
        pair = []
        for h in (low, low + half):
            of_head = jnp.concatenate(
                [
                    latent[q, pl.ds(h, seqs, stride=head_count), :]
                    for q in range(latent_dim // LANES)
                ],
                axis=1,
            )
            pair.append(dot(of_head.astype(BF16), value_up[h]))
        heads[y, c, :, low * VHEAD : (low + 1) * VHEAD] = jnp.concatenate(pair, axis=0).astype(
            BF16
        )

    pl.semaphore_wait(barrier, len(peers))

    mine = heads.at[y, c]
    for d in ys:
        send(mine, mine, head_send.at[d], head_recv.at[d], to_y(d))
    send(mine, mine, head_core_send.at[0], head_core_recv.at[0], partner)

    gain_row = gain_ref[...].astype(F32)
    router_all[c, g] = jnp.zeros(router_all.shape[2:], F32)
    router_all[c, g, :local_experts, :cols] = router_ref[...].astype(F32) * gain_row
    for d in xs:
        send(
            router_all.at[c, g], router_all.at[c, g], router_send.at[d], router_recv.at[d], to_x(d)
        )
    identity = (
        lax.broadcasted_iota(jnp.int32, (cols, cols), 0)
        == lax.broadcasted_iota(jnp.int32, (cols, cols), 1)
    ).astype(F32)
    gain_column = dot_nt(
        identity.astype(BF16), jnp.broadcast_to(gain_row, (LANES, cols)).astype(BF16)
    )
    loads[3].wait()
    for dst, first in ((weights_out, other * 2), (weights.at[c], c * 2)):
        dst[cols:, :] = jnp.zeros((wide_cols - cols, dst.shape[1]), BF16)
        for j in range(2):
            wide[...] = gate_up[first + j].astype(F32)
            for i in range(2):
                part = wide[pl.ds(i, cols, stride=2), :] * gain_column
                start = (2 * j + i) * LANES
                dst[:cols, start : start + LANES] = part.astype(BF16)
        if dst is weights_out:
            send(weights_out, weights.at[c], weight_send, weight_recv, partner)

    lane = lax.broadcasted_iota(jnp.int32, (block, LANES), 1)
    routes = routes_ref[...]
    slot_of = jnp.zeros(routes.shape, jnp.int32)
    for e in range(expert_slot_ref.shape[0]):
        slot_of = jnp.where(routes == e, expert_slot_ref[e], slot_of)
    used = cols - (wide_cols - LANES)
    slots = expert_slot_ref.shape[0]
    by_slot = jnp.zeros((slots, block), F32)
    slot_at = lax.broadcasted_iota(jnp.int32, (slots, block), 0)
    for k in range(routes.shape[0]):
        by_slot = by_slot + (slot_at == slot_of[k : k + 1, :]).astype(F32)
    same = lax.broadcasted_iota(jnp.int32, (block, block), 0) == lax.broadcasted_iota(
        jnp.int32, (block, block), 1
    )
    by_token = dot_nt(same.astype(F32), by_slot)
    place = lax.broadcasted_iota(jnp.int32, (slots, LANES), 1) - used
    place = (place == lax.broadcasted_iota(jnp.int32, (slots, LANES), 0)).astype(F32)
    extra[...] = dot(by_token, place)
    residual[:, wide_cols - LANES :] = jnp.zeros((block, LANES), F32)
    residual[:, :cols] = residual_ref[...].astype(F32)
    proj_out[:, :, wide_cols - LANES :] = jnp.zeros((nz, block, LANES), BF16)

    for d in ys:
        came = heads.at[at_y(-d), c]
        arrived(came, head_recv.at[d])
        send(came, came, head_core_send.at[d], head_core_recv.at[d], partner)
    loads[2].wait()
    for d in [0] + ys:
        arrived(heads.at[at_y(-d), other], head_core_recv.at[d])

    gathered = heads[...].reshape(ny * 2 * 2 * seqs, half * VHEAD)
    low_part = dot_nt(gathered, out_proj[:, : half * VHEAD]).reshape(ny * 2, 2, seqs, cols)
    high_part = dot_nt(gathered, out_proj[:, half * VHEAD :]).reshape(ny * 2, 2, seqs, cols)
    attn = (low_part[:, 0] + high_part[:, 1]).reshape(nz, block, cols)
    proj_out[:, :, :cols] = attn.astype(BF16)
    for d in zs:
        send(proj_out.at[at_z(d)], proj_in.at[t], proj_send.at[d], proj_recv.at[d], to_z(d))

    for d in xs:
        arrived(router_all.at[c, at_x(-d)], router_recv.at[d])
    send(router_all.at[c], router_all.at[c], router_send.at[0], router_recv.at[0], partner)
    arrived(weights.at[other], weight_recv)
    arrived(router_all.at[other], router_recv.at[0])
    pad = router_all.shape[2]
    slot_row = lax.broadcasted_iota(jnp.int32, (slots, nx * pad), 0)
    select = (
        lax.broadcasted_iota(jnp.int32, (slots, nx * pad), 1)
        == (slot_row // local_experts) * pad + lax.rem(slot_row, local_experts)
    ).astype(F32).astype(BF16)
    column = lax.broadcasted_iota(jnp.int32, (slots, wide_cols), 1)
    squares_at = (column == cols + slots) | (column == cols + slots + 1)
    for core in range(2):
        packed = router_all[core].reshape(nx * pad, wide_cols).astype(BF16)
        router_rows[core, :slots] = dot(select, packed).astype(BF16)
        router_rows[core, slots:] = squares_at.astype(F32).astype(BF16)

    total = residual[...] + proj_out[t].astype(F32)
    for d in zs:
        arrived(proj_in.at[at_z(-d)], proj_recv.at[d])
        total = total + proj_in[at_z(-d)].astype(F32)
    total = total.astype(BF16).astype(F32)
    stream[...] = total
    squares = jnp.sum(total * total, axis=1, keepdims=True)
    upper = squares.astype(BF16).astype(F32)
    marks = extra[...]
    marks = jnp.where(lane == used + slots, upper, marks)
    marks = jnp.where(lane == used + slots + 1, squares - upper, marks)
    rows[c, g, t, :, : wide_cols - LANES] = total[:, : wide_cols - LANES].astype(BF16)
    rows[c, g, t, :, wide_cols - LANES :] = (total[:, wide_cols - LANES :] + marks).astype(BF16)

    mine = rows.at[c, g, t]
    for d in zs:
        send(mine, mine, row_z_send.at[d], row_z_recv.at[d], to_z(d))
    for a in xs:
        send(mine, mine, row_x_send.at[a, 0], row_x_recv.at[a], to_x(a))
    for d in zs:
        came = rows.at[c, g, at_z(-d)]
        arrived(came, row_z_recv.at[d])
        for a in xs:
            send(came, came, row_x_send.at[a, d], row_x_recv.at[a], to_x(a))
    for a in [0] + xs:
        came = rows.at[c, at_x(-a)]
        if a:
            arrived(came, row_x_recv.at[a])
        send(came, came, row_core_send.at[a], row_core_recv.at[a], partner)
        arrived(rows.at[other, at_x(-a)], row_core_recv.at[a])
        of = at_x(-a)
        part = dot(rows[0, of].reshape(nz * block, wide_cols), weights[0])
        part = part + dot(rows[1, of].reshape(nz * block, wide_cols), weights[1])
        part_out[of] = part.astype(BF16).reshape(nz, block, part.shape[1])
        for d in ys:
            send(
                part_out.at[of, at_y(d)],
                part_in.at[y, of],
                part_send.at[d, a],
                part_recv.at[d],
                to_y(d),
            )

    chunk = nx * block
    tail = jnp.zeros((2 * slots, ny * chunk), F32)
    for core in range(2):
        by_owner = jnp.concatenate([rows[core, :, k].reshape(chunk, wide_cols) for k in range(nz)])
        tail = tail + dot_nt(router_rows[core], by_owner)
    lane_of = lax.broadcasted_iota(jnp.int32, (slots, LANES), 1)
    for j in range(ny * chunk // LANES):
        logits = tail[:slots, j * LANES : (j + 1) * LANES]
        sums = tail[slots:, j * LANES : (j + 1) * LANES]
        even = jnp.where(lane_of < chunk, logits, pltpu.roll(sums, chunk, 1))
        odd = jnp.where(lane_of < chunk, pltpu.roll(logits, chunk, 1), sums)
        tail_out[2 * j] = even.astype(BF16)
        tail_out[2 * j + 1] = odd.astype(BF16)
    for d in ys:
        send(tail_out.at[at_y(d)], tail_in.at[y], tail_send.at[d], tail_recv.at[d], to_y(d))

    total = part_out[:, y].astype(F32)
    tail = tail_out[y].astype(F32)
    for d in ys:
        arrived(part_in.at[at_y(-d)], part_recv.at[d])
        total = total + part_in[at_y(-d)].astype(F32)
    for d in ys:
        arrived(tail_in.at[at_y(-d)], tail_recv.at[d])
        tail = tail + tail_in[at_y(-d)].astype(F32)
    total = total.reshape(chunk, total.shape[2])
    down_at = lax.broadcasted_iota(jnp.int32, (chunk, LANES), 0)
    across = lax.broadcasted_iota(jnp.int32, (chunk, LANES), 1)
    logits = dot_nt((across == down_at).astype(F32), tail, lax.Precision.HIGHEST)
    sums = dot_nt((across == down_at + chunk).astype(F32), tail, lax.Precision.HIGHEST)
    inv_rms = lax.rsqrt(sums / width + EPSILON)
    marks = rows[c, :, y, :, wide_cols - LANES :].reshape(chunk, LANES).astype(F32)
    marks = pltpu.roll(marks, LANES - used, 1)[:, :slots]
    scores = jax.nn.sigmoid(logits * inv_rms) * marks
    shares = scores / jnp.sum(scores, axis=1, keepdims=True)
    slot_at = lax.broadcasted_iota(jnp.int32, (chunk, slots), 1)
    inv_rms = inv_rms[:, :1]
    for j in range(2):
        chosen = slot_at == g * local_experts + c * 2 + j
        share = jnp.sum(jnp.where(chosen, shares, 0.0), axis=1, keepdims=True)
        gate = total[:, 2 * j * LANES : (2 * j + 1) * LANES] * inv_rms
        up = total[:, (2 * j + 1) * LANES : (2 * j + 2) * LANES] * inv_rms
        value = jax.nn.silu(gate) * up * share
        hidden[c, y, :, j * LANES : (j + 1) * LANES] = value.astype(BF16)

    mine = hidden.at[c, y]
    for d in ys:
        send(mine, mine, hid_send.at[d], hid_recv.at[d], to_y(d))
    send(mine, mine, hid_core_send.at[0], hid_core_recv.at[0], partner)
    for load in loads[4:]:
        load.wait()
    down_out[:, :, :, wide_cols - LANES :] = jnp.zeros(down_out.shape[:3] + (LANES,), BF16)
    split = down.shape[1] // 2
    for d in [0] + ys:
        of = at_y(-d)
        if d:
            came = hidden.at[c, of]
            arrived(came, hid_recv.at[d])
            send(came, came, hid_core_send.at[d], hid_core_recv.at[d], partner)
        arrived(hidden.at[other, of], hid_core_recv.at[d])
        part = dot_nt(hidden[0, of], down[:, :split]) + dot_nt(hidden[1, of], down[:, split:])
        down_out[of, :, :, :cols] = part.astype(BF16).reshape(nx, block, cols)
        for a in xs:
            send(
                down_out.at[of, at_x(a)],
                down_in.at[a, of],
                down_send.at[a, d],
                down_recv.at[a, of],
                to_x(a),
            )

    for d in sorted(range(nz), key=lambda d: -min(d, nz - d)):
        of = at_z(d)
        total = down_out[of, g].astype(F32)
        for a in xs:
            arrived(down_in.at[a, of], down_recv.at[a, of])
            total = total + down_in[a, of].astype(F32)
        if d:
            sum_out[d] = total.astype(BF16)
            send(sum_out.at[d], sum_in.at[d], sum_send.at[d], sum_recv.at[d], to_z(d))
    total = total + stream[...]
    for d in zs:
        arrived(sum_in.at[d], sum_recv.at[d])
        total = total + sum_in[d].astype(F32)
    out_ref[...] = total[:, :cols].astype(BF16)

    for copy in sent:
        copy.wait_send()


def on_device(sizes, width, *arrays):
    (
        queries,
        latent_cache,
        lengths,
        value_up,
        out_proj,
        residual_in,
        norm_gain,
        router,
        gate_up,
        down_proj,
        routes,
        expert_slot,
    ) = arrays
    nx, ny, nz = sizes
    seqs, head_count, depth = queries.shape
    block, cols = residual_in.shape
    experts, _, _, units = gate_up.shape
    gate_up = gate_up.reshape(experts, cols * 2, units)
    down_proj = jnp.swapaxes(down_proj, 1, 2)
    latent_cache = jnp.swapaxes(latent_cache, 1, 2)
    out_proj = out_proj.T
    routes = routes.T
    gain = norm_gain.reshape(1, cols)
    wide_cols = -(-cols // LANES) * LANES
    latent_dim = value_up.shape[1]
    slots = expert_slot.shape[0]
    chunk = nx * block
    vmem = pl.BlockSpec(memory_space=pltpu.VMEM)
    smem = pl.BlockSpec(memory_space=pltpu.SMEM)
    anywhere = pl.BlockSpec(memory_space=pltpu.HBM)
    sem = pltpu.SemaphoreType.DMA
    scratch = [
        pltpu.VMEM(latent_cache.shape, BF16),
        pltpu.VMEM(value_up.shape, BF16),
        pltpu.VMEM(out_proj.shape, BF16),
        pltpu.VMEM(gate_up.shape, BF16),
        pltpu.VMEM((cols, experts * units), BF16),
        pltpu.VMEM((latent_dim // LANES, seqs * head_count, LANES), F32),
        pltpu.VMEM((ny, 2, 2 * seqs, head_count // 2 * VHEAD), BF16),
        pltpu.VMEM((nz, block, wide_cols), BF16),
        pltpu.VMEM((nz, block, wide_cols), BF16),
        pltpu.VMEM((block, wide_cols), F32),
        pltpu.VMEM((block, LANES), F32),
        pltpu.VMEM((block, wide_cols), F32),
        pltpu.VMEM((2, nx, nz, block, wide_cols), BF16),
        pltpu.VMEM((cols * 2, units), F32),
        pltpu.VMEM((2, wide_cols, 4 * units), BF16),
        pltpu.VMEM((wide_cols, 4 * units), BF16),
        pltpu.VMEM((2, nx, 8, wide_cols), F32),
        pltpu.VMEM((2, 2 * slots, wide_cols), BF16),
        pltpu.VMEM((nx, nz, block, 4 * units), BF16),
        pltpu.VMEM((ny, nx, block, 4 * units), BF16),
        pltpu.VMEM((ny, slots, LANES), BF16),
        pltpu.VMEM((ny, slots, LANES), BF16),
        pltpu.VMEM((2, ny, chunk, 2 * units), BF16),
        pltpu.VMEM((ny, nx, block, wide_cols), BF16),
        pltpu.VMEM((nx, ny, block, wide_cols), BF16),
        pltpu.VMEM((nz, block, wide_cols), BF16),
        pltpu.VMEM((nz, block, wide_cols), BF16),
        sem((4 + experts,)),
        sem((ny,)),
        sem((ny,)),
        sem((ny,)),
        sem((ny,)),
        sem,
        sem,
        sem((nx,)),
        sem((nx,)),
        sem((nz,)),
        sem((nz,)),
        sem((nz,)),
        sem((nz,)),
        sem((nx, nz)),
        sem((nx,)),
        sem((nx,)),
        sem((nx,)),
        sem((ny, nx)),
        sem((ny,)),
        sem((ny,)),
        sem((ny,)),
        sem((ny,)),
        sem((ny,)),
        sem((ny,)),
        sem((ny,)),
        sem((nx, ny)),
        sem((nx, ny)),
        sem((nz,)),
        sem((nz,)),
    ]
    return pl.pallas_call(
        functools.partial(kernel, sizes, width),
        out_shape=jax.ShapeDtypeStruct((block, cols), BF16),
        in_specs=[smem, smem, vmem, vmem, vmem, vmem, vmem] + [anywhere] * 5,
        out_specs=vmem,
        scratch_shapes=scratch,
        name="decode_layer",
        compiler_params=pltpu.CompilerParams(
            collective_id=0, has_side_effects=True, vmem_limit_bytes=60 * 2**20
        ),
    )(
        lengths,
        expert_slot,
        queries,
        residual_in,
        gain,
        router,
        routes,
        latent_cache,
        value_up,
        out_proj,
        gate_up,
        down_proj,
    )


def solution(mesh):
    in_specs = (
        P(("grp", "dp"), "tensor", None),
        P(("grp", "dp"), None, None),
        P(("grp", "dp")),
        P("tensor", None, None),
        P("tensor", "dp"),
        P(("grp", "tensor"), "dp"),
        P("dp"),
        P("grp", "dp"),
        P("grp", "dp", None, "tensor"),
        P("grp", "tensor", "dp"),
        P(("grp", "tensor"), None),
        P(),
    )
    out_specs = P(("grp", "tensor"), "dp")
    sizes = (mesh.shape["grp"], mesh.shape["dp"] // 2, mesh.shape["tensor"])

    def whole(*arrays):
        width = arrays[5].shape[1]
        return jax.shard_map(
            functools.partial(on_device, sizes, width),
            mesh=mesh,
            in_specs=in_specs,
            out_specs=out_specs,
            check_vma=False,
        )(*arrays)

    return whole
```

```python
import functools

import jax
import jax.numpy as jnp
from jax import lax
from jax.experimental import pallas as pl
from jax.experimental.pallas import tpu as pltpu
from jax.sharding import PartitionSpec as P

ROPE = 64
VHEAD = 128
EPSILON = 1e-06
MESH = pl.DeviceIdType.MESH
BF16 = jnp.bfloat16
F32 = jnp.float32
LANES = 128


def dot(a, b):
    return jnp.dot(a, b, preferred_element_type=F32)


def dot_nt(a, b, precision=None):
    return lax.dot_general(
        a, b, (((1,), (1,)), ((), ())), preferred_element_type=F32, precision=precision
    )


def near_first(count):
    return sorted(range(1, count), key=lambda d: (min(d, count - d), d))


def kernel(
    sizes,
    width,
    lengths_hbm,
    expert_slot_hbm,
    queries_hbm,
    residual_hbm,
    gain_hbm,
    router_hbm,
    routes_hbm,
    cache_hbm,
    value_up_hbm,
    out_proj_hbm,
    gate_up_hbm,
    down_hbm,
    out_ref,
    lengths_ref,
    expert_slot_ref,
    queries_ref,
    residual_ref,
    gain_ref,
    router_ref,
    routes_ref,
    cache,
    value_up,
    out_proj,
    gate_up,
    down,
    latent,
    heads,
    proj_out,
    proj_in,
    residual,
    extra,
    stream,
    rows,
    wide,
    weights,
    weights_out,
    router_all,
    router_rows,
    part_out,
    part_in,
    tail_out,
    tail_in,
    hidden,
    down_out,
    down_in,
    sum_out,
    sum_in,
    load_sem,
    small_sem,
    head_send,
    head_recv,
    head_core_send,
    head_core_recv,
    weight_send,
    weight_recv,
    router_send,
    router_recv,
    proj_send,
    proj_recv,
    row_z_send,
    row_z_recv,
    row_x_send,
    row_x_recv,
    row_core_send,
    row_core_recv,
    part_send,
    part_recv,
    tail_send,
    tail_recv,
    hid_send,
    hid_recv,
    hid_core_send,
    hid_core_recv,
    down_send,
    down_recv,
    sum_send,
    sum_recv,
):
    nx, ny, nz = sizes
    g = lax.axis_index("grp")
    dp = lax.axis_index("dp")
    t = lax.axis_index("tensor")
    y = dp // 2
    c = lax.rem(dp, 2)
    other = 1 - c
    cols = residual_ref.shape[1]
    block = residual_ref.shape[0]
    wide_cols = stream.shape[1]
    seqs, head_count, depth = queries_ref.shape
    latent_dim = value_up.shape[1]
    local_experts = router_ref.shape[0]
    ys, zs = near_first(ny), near_first(nz)
    xs = [1, 3, 2]
    far_ys, far_zs = ys[::-1], zs[::-1]

    def at_x(code):
        return [g, g + 1 - 2 * lax.rem(g, 2), lax.rem(g + 2, nx), nx - 1 - g][code]

    def at_y(d):
        return lax.rem(y + ny + d, ny)

    def at_z(d):
        return lax.rem(t + nz + d, nz)

    def to_x(d):
        return (at_x(d), dp, t)

    def to_y(d):
        return (g, at_y(d) * 2 + c, t)

    def to_z(d):
        return (g, dp, at_z(d))

    partner = (g, y * 2 + other, t)
    sent = []

    def send(src, dst, send_sem, recv_sem, device):
        copy = pltpu.make_async_remote_copy(
            src_ref=src,
            dst_ref=dst,
            send_sem=send_sem,
            recv_sem=recv_sem,
            device_id=device,
            device_id_type=MESH,
        )
        copy.start()
        sent.append(copy)

    def arrived(dst, recv_sem):
        pltpu.make_async_remote_copy(
            src_ref=dst,
            dst_ref=dst,
            send_sem=load_sem.at[0],
            recv_sem=recv_sem,
            device_id=partner,
            device_id_type=MESH,
        ).wait_recv()

    barrier = pltpu.get_barrier_semaphore()
    peers = [partner] + [to_y(d) for d in ys] + [to_z(d) for d in zs] + [to_x(d) for d in xs]
    for device in peers:
        pl.semaphore_signal(barrier, inc=1, device_id=device, device_id_type=MESH)

    small = [
        pltpu.make_async_copy(src, dst, small_sem.at[i])
        for i, (src, dst) in enumerate(
            [
                (lengths_hbm, lengths_ref),
                (queries_hbm, queries_ref),
                (expert_slot_hbm, expert_slot_ref),
                (gain_hbm, gain_ref),
                (router_hbm, router_ref),
                (routes_hbm, routes_ref),
                (residual_hbm, residual_ref),
            ]
        )
    ]

    loads = [
        pltpu.make_async_copy(src, dst, load_sem.at[i])
        for i, (src, dst) in enumerate(
            [
                (cache_hbm, cache),
                (value_up_hbm, value_up),
                (out_proj_hbm, out_proj),
                (gate_up_hbm, gate_up),
            ]
            + [
                (down_hbm.at[e], down.at[:, pl.ds(e * down_hbm.shape[2], down_hbm.shape[2])])
                for e in range(local_experts)
            ]
        )
    ]
    for load in small[:2] + loads[:1] + small[2:] + loads[1:]:
        load.start()

    score_scale = (VHEAD + ROPE) ** (-0.5)
    for load in small[:2]:
        load.wait()
    loads[0].wait()
    for n in range(seqs):
        scores = dot(queries_ref[n], cache[n]) * score_scale
        positions = lax.broadcasted_iota(jnp.int32, scores.shape, 1)
        scores = jnp.where(positions < lengths_ref[n], scores, -1e30)
        exps = jnp.exp(scores - jnp.max(scores, axis=1, keepdims=True))
        probs = (exps / jnp.sum(exps, axis=1, keepdims=True)).astype(BF16)
        of_seq = dot_nt(probs, cache[n, :latent_dim, :])
        for q in range(latent_dim // LANES):
            latent[q, n * head_count : (n + 1) * head_count, :] = of_seq[
                :, q * LANES : (q + 1) * LANES
            ]
    loads[1].wait()
    half = head_count // 2
    for low in range(half):
        pair = []
        for h in (low, low + half):
            of_head = jnp.concatenate(
                [
                    latent[q, pl.ds(h, seqs, stride=head_count), :]
                    for q in range(latent_dim // LANES)
                ],
                axis=1,
            )
            pair.append(dot(of_head.astype(BF16), value_up[h]))
        heads[y, c, :, low * VHEAD : (low + 1) * VHEAD] = jnp.concatenate(pair, axis=0).astype(
            BF16
        )

    pl.semaphore_wait(barrier, len(peers))

    mine = heads.at[y, c]
    for d in far_ys:
        send(mine, mine, head_send.at[d], head_recv.at[d], to_y(d))
    send(mine, mine, head_core_send.at[0], head_core_recv.at[0], partner)

    for load in small[2:]:
        load.wait()
    gain_row = gain_ref[...].astype(F32)[None, :]
    router_all[c, g] = jnp.zeros(router_all.shape[2:], F32)
    router_all[c, g, :local_experts, :cols] = router_ref[...].astype(F32) * gain_row
    for d in xs:
        send(
            router_all.at[c, g], router_all.at[c, g], router_send.at[d], router_recv.at[d], to_x(d)
        )
    identity = (
        lax.broadcasted_iota(jnp.int32, (cols, cols), 0)
        == lax.broadcasted_iota(jnp.int32, (cols, cols), 1)
    ).astype(F32)
    gain_column = dot_nt(
        identity.astype(BF16), jnp.broadcast_to(gain_row, (LANES, cols)).astype(BF16)
    )
    loads[3].wait()
    for dst, first in ((weights_out, other * 2), (weights.at[c], c * 2)):
        dst[cols:, :] = jnp.zeros((wide_cols - cols, dst.shape[1]), BF16)
        for j in range(2):
            wide[...] = gate_up[first + j].astype(F32)
            for i in range(2):
                part = wide[pl.ds(i, cols, stride=2), :] * gain_column
                start = (2 * j + i) * LANES
                dst[:cols, start : start + LANES] = part.astype(BF16)
        if dst is weights_out:
            send(weights_out, weights.at[c], weight_send, weight_recv, partner)

    lane = lax.broadcasted_iota(jnp.int32, (block, LANES), 1)
    routes = routes_ref[...]
    slot_of = jnp.zeros(routes.shape, jnp.int32)
    for e in range(expert_slot_ref.shape[0]):
        slot_of = jnp.where(routes == e, expert_slot_ref[e], slot_of)
    used = cols - (wide_cols - LANES)
    slots = expert_slot_ref.shape[0]
    by_slot = jnp.zeros((slots, block), F32)
    slot_at = lax.broadcasted_iota(jnp.int32, (slots, block), 0)
    for k in range(routes.shape[0]):
        by_slot = by_slot + (slot_at == slot_of[k : k + 1, :]).astype(F32)
    same = lax.broadcasted_iota(jnp.int32, (block, block), 0) == lax.broadcasted_iota(
        jnp.int32, (block, block), 1
    )
    by_token = dot_nt(same.astype(F32), by_slot)
    place = lax.broadcasted_iota(jnp.int32, (slots, LANES), 1) - used
    place = (place == lax.broadcasted_iota(jnp.int32, (slots, LANES), 0)).astype(F32)
    extra[...] = dot(by_token, place)
    residual[:, wide_cols - LANES :] = jnp.zeros((block, LANES), F32)
    residual[:, :cols] = residual_ref[...].astype(F32)
    proj_out[:, :, wide_cols - LANES :] = jnp.zeros((nz, block, LANES), BF16)

    for d in ys:
        came = heads.at[at_y(-d), c]
        arrived(came, head_recv.at[d])
        send(came, came, head_core_send.at[d], head_core_recv.at[d], partner)
    loads[2].wait()
    for d in [0] + ys:
        arrived(heads.at[at_y(-d), other], head_core_recv.at[d])

    gathered = heads[...].reshape(ny * 2 * 2 * seqs, half * VHEAD)
    low_part = dot_nt(gathered, out_proj[:, : half * VHEAD]).reshape(ny * 2, 2, seqs, cols)
    high_part = dot_nt(gathered, out_proj[:, half * VHEAD :]).reshape(ny * 2, 2, seqs, cols)
    attn = (low_part[:, 0] + high_part[:, 1]).reshape(nz, block, cols)
    proj_out[:, :, :cols] = attn.astype(BF16)
    for d in far_zs:
        send(proj_out.at[at_z(d)], proj_in.at[t], proj_send.at[d], proj_recv.at[d], to_z(d))

    for d in xs:
        arrived(router_all.at[c, at_x(d)], router_recv.at[d])
    send(router_all.at[c], router_all.at[c], router_send.at[0], router_recv.at[0], partner)
    arrived(weights.at[other], weight_recv)
    arrived(router_all.at[other], router_recv.at[0])
    pad = router_all.shape[2]
    slot_row = lax.broadcasted_iota(jnp.int32, (slots, nx * pad), 0)
    select = (
        lax.broadcasted_iota(jnp.int32, (slots, nx * pad), 1)
        == (slot_row // local_experts) * pad + lax.rem(slot_row, local_experts)
    ).astype(F32).astype(BF16)
    column = lax.broadcasted_iota(jnp.int32, (slots, wide_cols), 1)
    squares_at = (column == cols + slots) | (column == cols + slots + 1)
    for core in range(2):
        packed = router_all[core].reshape(nx * pad, wide_cols).astype(BF16)
        router_rows[core, :slots] = dot(select, packed).astype(BF16)
        router_rows[core, slots:] = squares_at.astype(F32).astype(BF16)

    total = residual[...] + proj_out[t].astype(F32)
    for d in zs:
        arrived(proj_in.at[at_z(-d)], proj_recv.at[d])
        total = total + proj_in[at_z(-d)].astype(F32)
    total = total.astype(BF16).astype(F32)
    stream[...] = total
    squares = jnp.sum(total * total, axis=1, keepdims=True)
    upper = squares.astype(BF16).astype(F32)
    marks = extra[...]
    marks = jnp.where(lane == used + slots, upper, marks)
    marks = jnp.where(lane == used + slots + 1, squares - upper, marks)
    rows[c, g, t, :, : wide_cols - LANES] = total[:, : wide_cols - LANES].astype(BF16)
    rows[c, g, t, :, wide_cols - LANES :] = (total[:, wide_cols - LANES :] + marks).astype(BF16)

    mine = rows.at[c, g, t]
    for d in far_zs:
        send(mine, mine, row_z_send.at[d], row_z_recv.at[d], to_z(d))
    for a in (2, 1, 3):
        send(mine, mine, row_x_send.at[a, 0], row_x_recv.at[a], to_x(a))
    for d in zs:
        came = rows.at[c, g, at_z(-d)]
        arrived(came, row_z_recv.at[d])
        for a in (2, 1, 3):
            send(came, came, row_x_send.at[a, d], row_x_recv.at[a], to_x(a))
    def pass_rows(a):
        came = rows.at[c, at_x(a)]
        if a:
            arrived(came, row_x_recv.at[a])
        send(came, came, row_core_send.at[a], row_core_recv.at[a], partner)

    def multiply_rows(a):
        of = at_x(a)
        part = dot(rows[c, of].reshape(nz * block, wide_cols), weights[c])
        arrived(rows.at[other, of], row_core_recv.at[a])
        part = part + dot(rows[other, of].reshape(nz * block, wide_cols), weights[other])
        part_out[of] = part.astype(BF16).reshape(nz, block, part.shape[1])
        of_half, place = [(0, 0), (1, 0), (0, 1), (1, 1)][a]
        for d in far_ys:
            send(
                part_out.at[of, at_y(d)],
                part_in.at[of_half, y, place],
                part_send.at[d, a],
                part_recv.at[of_half, d],
                to_y(d),
            )

    chunk = 2 * block
    halves = ((0, 2), (1, 3))
    per_tile = LANES // chunk

    def send_tail(h):
        missing = max(LANES - nz * chunk, 0)
        tail = jnp.zeros((2 * slots, nz * chunk + missing), F32)
        for core in range(2):
            by_owner = jnp.concatenate(
                [
                    rows[core, at_x(code)].reshape(nz, 1, block, wide_cols)
                    for code in halves[h]
                ],
                axis=1,
            ).reshape(nz * chunk, wide_cols)
            if missing:
                by_owner = jnp.concatenate([by_owner, jnp.zeros((missing, wide_cols), BF16)])
            tail = tail + dot_nt(router_rows[core], by_owner)
        lane_of = lax.broadcasted_iota(jnp.int32, (slots, LANES), 1)
        for q in range(ny):
            tile = slice(q // per_tile * LANES, (q // per_tile + 1) * LANES)
            turn = LANES - q % per_tile * chunk
            logits = pltpu.roll(tail[:slots, tile], turn % LANES, 1)
            sums = pltpu.roll(tail[slots:, tile], (turn + chunk) % LANES, 1)
            tail_out[h, q] = jnp.where(lane_of < chunk, logits, sums).astype(BF16)
        for d in far_ys:
            send(
                tail_out.at[h, at_y(d)],
                tail_in.at[h, y],
                tail_send.at[h, d],
                tail_recv.at[h, d],
                to_y(d),
            )

    pass_rows(0)
    multiply_rows(0)
    pass_rows(2)
    pass_rows(1)
    multiply_rows(2)
    send_tail(0)
    pass_rows(3)
    multiply_rows(1)
    multiply_rows(3)
    send_tail(1)

    down_at = lax.broadcasted_iota(jnp.int32, (chunk, LANES), 0)
    across = lax.broadcasted_iota(jnp.int32, (chunk, LANES), 1)
    slot_at = lax.broadcasted_iota(jnp.int32, (chunk, slots), 1)

    def find_hidden(h):
        tail = tail_out[h, y].astype(F32)
        total = jnp.concatenate([part_out[at_x(code), y] for code in halves[h]]).astype(F32)
        for d in ys:
            of = at_y(-d)
            arrived(tail_in.at[h, of], tail_recv.at[h, d])
            tail = tail + tail_in[h, of].astype(F32)
        for d in ys:
            of = at_y(-d)
            arrived(part_in.at[h, of], part_recv.at[h, d])
            total = total + part_in[h, of].reshape(total.shape).astype(F32)
        logits = dot_nt((across == down_at).astype(F32), tail, lax.Precision.HIGHEST)
        sums = dot_nt((across == down_at + chunk).astype(F32), tail, lax.Precision.HIGHEST)
        inv_rms = lax.rsqrt(sums / width + EPSILON)
        marks = jnp.concatenate(
            [rows[c, at_x(code), y, :, wide_cols - LANES :] for code in halves[h]]
        ).astype(F32)
        marks = pltpu.roll(marks, LANES - used, 1)[:, :slots]
        scores = jax.nn.sigmoid(logits * inv_rms) * marks
        shares = scores / jnp.sum(scores, axis=1, keepdims=True)
        inv_rms = inv_rms[:, :1]
        for j in range(2):
            chosen = slot_at == g * local_experts + c * 2 + j
            share = jnp.sum(jnp.where(chosen, shares, 0.0), axis=1, keepdims=True)
            gate = total[:, 2 * j * LANES : (2 * j + 1) * LANES] * inv_rms
            up = total[:, (2 * j + 1) * LANES : (2 * j + 2) * LANES] * inv_rms
            value = jax.nn.silu(gate) * up * share
            hidden[h, c, y, :, j * LANES : (j + 1) * LANES] = value.astype(BF16)
        mine = hidden.at[h, c, y]
        for d in ys:
            send(mine, mine, hid_send.at[h, d], hid_recv.at[h, d], to_y(d))
        send(mine, mine, hid_core_send.at[h, 0], hid_core_recv.at[h, 0], partner)

    down_out[:, :, :, :, wide_cols - LANES :] = jnp.zeros(down_out.shape[:4] + (LANES,), BF16)
    find_hidden(0)
    find_hidden(1)
    for load in loads[4:]:
        load.wait()
    split = down.shape[1] // 2

    def pass_hidden(h, d):
        if d:
            came = hidden.at[h, c, at_y(-d)]
            arrived(came, hid_recv.at[h, d])
            send(came, came, hid_core_send.at[h, d], hid_core_recv.at[h, d], partner)

    def multiply_hidden(h, d):
        of = at_y(-d)
        arrived(hidden.at[h, other, of], hid_core_recv.at[h, d])
        part = dot_nt(hidden[h, 0, of], down[:, :split])
        part = part + dot_nt(hidden[h, 1, of], down[:, split:])
        down_out[h, of, :, :, :cols] = part.astype(BF16).reshape(2, block, cols)
        for place, code in enumerate(halves[h]):
            if code:
                send(
                    down_out.at[h, of, place],
                    down_in.at[code, of],
                    down_send.at[code, d],
                    down_recv.at[code, d],
                    to_x(code),
                )

    def to_owner(d):
        return pltpu.make_async_remote_copy(
            src_ref=sum_out.at[at_y(-d)],
            dst_ref=sum_in.at[t],
            send_sem=sum_send.at[d],
            recv_sem=sum_recv.at[t],
            device_id=(g, dp, at_y(-d)),
            device_id_type=MESH,
        )

    def add_groups(d):
        of = at_y(-d)
        total = down_out[0, of, 0].astype(F32)
        for a in (2, 1, 3):
            arrived(down_in.at[a, of], down_recv.at[a, d])
            total = total + down_in[a, of].astype(F32)
        sum_out[of] = total.astype(BF16)

        @pl.when(of != t)
        def _():
            to_owner(d).start()

    order = [0] + ys
    steps = [(h, d) for h in range(2) for d in order]
    pass_hidden(*steps[0])
    for i, (h, d) in enumerate(steps):
        if i + 1 < len(steps):
            pass_hidden(*steps[i + 1])
        multiply_hidden(h, d)
        if i - ny >= 2:
            add_groups(order[i - ny - 2])
    for d in order[max(ny - 2, 0) :]:
        add_groups(d)
    total = stream[...] + sum_out[t].astype(F32)
    for d in zs:
        of = at_z(-d)
        arrived(sum_in.at[of], sum_recv.at[of])
        total = total + sum_in[of].astype(F32)
    out_ref[...] = total[:, :cols].astype(BF16)

    for d in order:

        @pl.when(at_y(-d) != t)
        def _():
            to_owner(d).wait_send()

    for copy in sent:
        copy.wait_send()


def on_device(sizes, width, *arrays):
    (
        queries,
        latent_cache,
        lengths,
        value_up,
        out_proj,
        residual_in,
        norm_gain,
        router,
        gate_up,
        down_proj,
        routes,
        expert_slot,
    ) = arrays
    nx, ny, nz = sizes
    seqs, head_count, depth = queries.shape
    block, cols = residual_in.shape
    experts, _, _, units = gate_up.shape
    gate_up = gate_up.reshape(experts, cols * 2, units)
    down_proj = jnp.swapaxes(down_proj, 1, 2)
    latent_cache = jnp.swapaxes(latent_cache, 1, 2)
    out_proj = out_proj.T
    routes = routes.T
    wide_cols = -(-cols // LANES) * LANES
    latent_dim = value_up.shape[1]
    slots = expert_slot.shape[0]
    vmem = pl.BlockSpec(memory_space=pltpu.VMEM)
    anywhere = pl.BlockSpec(memory_space=pltpu.HBM)
    sem = pltpu.SemaphoreType.DMA
    scratch = [
        pltpu.SMEM(lengths.shape, jnp.int32),
        pltpu.SMEM(expert_slot.shape, jnp.int32),
        pltpu.VMEM(queries.shape, BF16),
        pltpu.VMEM(residual_in.shape, BF16),
        pltpu.VMEM(norm_gain.shape, BF16),
        pltpu.VMEM(router.shape, BF16),
        pltpu.VMEM(routes.shape, jnp.int32),
        pltpu.VMEM(latent_cache.shape, BF16),
        pltpu.VMEM(value_up.shape, BF16),
        pltpu.VMEM(out_proj.shape, BF16),
        pltpu.VMEM(gate_up.shape, BF16),
        pltpu.VMEM((cols, experts * units), BF16),
        pltpu.VMEM((latent_dim // LANES, seqs * head_count, LANES), F32),
        pltpu.VMEM((ny, 2, 2 * seqs, head_count // 2 * VHEAD), BF16),
        pltpu.VMEM((nz, block, wide_cols), BF16),
        pltpu.VMEM((nz, block, wide_cols), BF16),
        pltpu.VMEM((block, wide_cols), F32),
        pltpu.VMEM((block, LANES), F32),
        pltpu.VMEM((block, wide_cols), F32),
        pltpu.VMEM((2, nx, nz, block, wide_cols), BF16),
        pltpu.VMEM((cols * 2, units), F32),
        pltpu.VMEM((2, wide_cols, 4 * units), BF16),
        pltpu.VMEM((wide_cols, 4 * units), BF16),
        pltpu.VMEM((2, nx, 8, wide_cols), F32),
        pltpu.VMEM((2, 2 * slots, wide_cols), BF16),
        pltpu.VMEM((nx, nz, block, 4 * units), BF16),
        pltpu.VMEM((2, ny, 2, block, 4 * units), BF16),
        pltpu.VMEM((2, ny, slots, LANES), BF16),
        pltpu.VMEM((2, ny, slots, LANES), BF16),
        pltpu.VMEM((2, 2, ny, 2 * block, 2 * units), BF16),
        pltpu.VMEM((2, ny, 2, block, wide_cols), BF16),
        pltpu.VMEM((nx, ny, block, wide_cols), BF16),
        pltpu.VMEM((nz, block, wide_cols), BF16),
        pltpu.VMEM((nz, block, wide_cols), BF16),
        sem((4 + experts,)),
        sem((7,)),
        sem((ny,)),
        sem((ny,)),
        sem((ny,)),
        sem((ny,)),
        sem,
        sem,
        sem((nx,)),
        sem((nx,)),
        sem((nz,)),
        sem((nz,)),
        sem((nz,)),
        sem((nz,)),
        sem((nx, nz)),
        sem((nx,)),
        sem((nx,)),
        sem((nx,)),
        sem((ny, nx)),
        sem((2, ny)),
        sem((2, ny)),
        sem((2, ny)),
        sem((2, ny)),
        sem((2, ny)),
        sem((2, ny)),
        sem((2, ny)),
        sem((nx, ny)),
        sem((nx, ny)),
        sem((nz,)),
        sem((nz,)),
    ]
    return pl.pallas_call(
        functools.partial(kernel, sizes, width),
        out_shape=jax.ShapeDtypeStruct((block, cols), BF16),
        in_specs=[anywhere] * 12,
        out_specs=vmem,
        scratch_shapes=scratch,
        name="decode_layer",
        compiler_params=pltpu.CompilerParams(
            collective_id=0, has_side_effects=True, vmem_limit_bytes=60 * 2**20
        ),
    )(
        lengths,
        expert_slot,
        queries,
        residual_in,
        norm_gain,
        router,
        routes,
        latent_cache,
        value_up,
        out_proj,
        gate_up,
        down_proj,
    )


def solution(mesh):
    in_specs = (
        P(("grp", "dp"), "tensor", None),
        P(("grp", "dp"), None, None),
        P(("grp", "dp")),
        P("tensor", None, None),
        P("tensor", "dp"),
        P(("grp", "tensor"), "dp"),
        P("dp"),
        P("grp", "dp"),
        P("grp", "dp", None, "tensor"),
        P("grp", "tensor", "dp"),
        P(("grp", "tensor"), None),
        P(),
    )
    out_specs = P(("grp", "tensor"), "dp")
    sizes = (mesh.shape["grp"], mesh.shape["dp"] // 2, mesh.shape["tensor"])

    def whole(*arrays):
        width = arrays[5].shape[1]
        return jax.shard_map(
            functools.partial(on_device, sizes, width),
            mesh=mesh,
            in_specs=in_specs,
            out_specs=out_specs,
            check_vma=False,
        )(*arrays)

    return whole
```

```python
import functools

import jax
import jax.numpy as jnp
from jax import lax
from jax.experimental import pallas as pl
from jax.experimental.pallas import tpu as pltpu
from jax.sharding import PartitionSpec as P

ROPE = 64
VHEAD = 128
EPSILON = 1e-06
MESH = pl.DeviceIdType.MESH
BF16 = jnp.bfloat16
F32 = jnp.float32
LANES = 128


def dot(a, b):
    return jnp.dot(a, b, preferred_element_type=F32)


def dot_nt(a, b, precision=None):
    return lax.dot_general(
        a, b, (((1,), (1,)), ((), ())), preferred_element_type=F32, precision=precision
    )


def near_first(count):
    return sorted(range(1, count), key=lambda d: (min(d, count - d), d))


def kernel(
    sizes,
    width,
    lengths_hbm,
    expert_slot_hbm,
    queries_hbm,
    residual_hbm,
    gain_hbm,
    router_hbm,
    routes_hbm,
    cache_hbm,
    value_up_hbm,
    out_proj_hbm,
    gate_up_hbm,
    down_hbm,
    out_ref,
    lengths_ref,
    expert_slot_ref,
    queries_ref,
    residual_ref,
    gain_ref,
    router_ref,
    routes_ref,
    cache,
    value_up,
    out_proj,
    gate_up,
    down,
    latent,
    heads,
    proj_out,
    proj_in,
    residual,
    extra,
    stream,
    rows,
    wide,
    weights,
    weights_out,
    router_all,
    router_rows,
    part_out,
    part_in,
    tail_out,
    tail_in,
    hidden,
    down_out,
    down_in,
    sum_out,
    sum_in,
    load_sem,
    small_sem,
    head_send,
    head_recv,
    head_core_send,
    head_core_recv,
    weight_send,
    weight_recv,
    router_send,
    router_recv,
    proj_send,
    proj_recv,
    row_z_send,
    row_z_recv,
    row_x_send,
    row_x_recv,
    row_core_send,
    row_core_recv,
    part_send,
    part_recv,
    tail_send,
    tail_recv,
    hid_send,
    hid_recv,
    hid_core_send,
    hid_core_recv,
    down_send,
    down_recv,
    sum_send,
    sum_recv,
):
    nx, ny, nz = sizes
    g = lax.axis_index("grp")
    dp = lax.axis_index("dp")
    t = lax.axis_index("tensor")
    y = dp // 2
    c = lax.rem(dp, 2)
    other = 1 - c
    cols = residual_ref.shape[1]
    block = residual_ref.shape[0]
    wide_cols = stream.shape[1]
    seqs, head_count, depth = queries_ref.shape
    latent_dim = value_up.shape[1]
    local_experts = router_ref.shape[0]
    ys, zs = near_first(ny), near_first(nz)
    xs = [1, 3, 2]
    far_ys, far_zs = ys[::-1], zs[::-1]

    def at_x(code):
        return [g, g + 1 - 2 * lax.rem(g, 2), lax.rem(g + 2, nx), nx - 1 - g][code]

    def at_y(d):
        return lax.rem(y + ny + d, ny)

    def at_z(d):
        return lax.rem(t + nz + d, nz)

    def to_x(d):
        return (at_x(d), dp, t)

    def to_y(d):
        return (g, at_y(d) * 2 + c, t)

    def to_z(d):
        return (g, dp, at_z(d))

    partner = (g, y * 2 + other, t)
    sent = []

    def send(src, dst, send_sem, recv_sem, device):
        copy = pltpu.make_async_remote_copy(
            src_ref=src,
            dst_ref=dst,
            send_sem=send_sem,
            recv_sem=recv_sem,
            device_id=device,
            device_id_type=MESH,
        )
        copy.start()
        sent.append(copy)

    def arrived(dst, recv_sem):
        pltpu.make_async_remote_copy(
            src_ref=dst,
            dst_ref=dst,
            send_sem=load_sem.at[0],
            recv_sem=recv_sem,
            device_id=partner,
            device_id_type=MESH,
        ).wait_recv()

    barrier = pltpu.get_barrier_semaphore()
    peers = [partner] + [to_y(d) for d in ys] + [to_z(d) for d in zs] + [to_x(d) for d in xs]
    for device in peers:
        pl.semaphore_signal(barrier, inc=1, device_id=device, device_id_type=MESH)

    small = [
        pltpu.make_async_copy(src, dst, small_sem.at[i])
        for i, (src, dst) in enumerate(
            [
                (lengths_hbm, lengths_ref),
                (queries_hbm, queries_ref),
                (expert_slot_hbm, expert_slot_ref),
                (gain_hbm, gain_ref),
                (router_hbm, router_ref),
                (routes_hbm, routes_ref),
                (residual_hbm, residual_ref),
            ]
        )
    ]

    loads = [
        pltpu.make_async_copy(src, dst, load_sem.at[i])
        for i, (src, dst) in enumerate(
            [
                (cache_hbm, cache),
                (value_up_hbm, value_up),
                (out_proj_hbm, out_proj),
                (gate_up_hbm, gate_up),
            ]
            + [
                (down_hbm.at[e], down.at[:, pl.ds(e * down_hbm.shape[2], down_hbm.shape[2])])
                for e in range(local_experts)
            ]
        )
    ]
    for load in small[:2] + loads[:1]:
        load.start()

    score_scale = (VHEAD + ROPE) ** (-0.5)
    for load in small[:2] + loads[:1]:
        load.wait()
    for load in loads[1:2] + small[2:] + loads[2:]:
        load.start()
    scores = []
    positions = lax.broadcasted_iota(jnp.int32, (head_count, cache.shape[2]), 1)
    for n in range(seqs):
        of_seq = dot(queries_ref[n], cache[n]) * score_scale
        scores.append(jnp.where(positions < lengths_ref[n], of_seq, -1e30))
    scores = jnp.concatenate(scores)
    exps = jnp.exp(scores - jnp.max(scores, axis=1, keepdims=True))
    probs = exps / jnp.sum(exps, axis=1, keepdims=True)
    for n in range(seqs):
        of_heads = slice(n * head_count, (n + 1) * head_count)
        of_seq = dot_nt(probs[of_heads].astype(BF16), cache[n, :latent_dim, :])
        for q in range(latent_dim // LANES):
            latent[q, of_heads, :] = of_seq[:, q * LANES : (q + 1) * LANES]
    loads[1].wait()
    half = head_count // 2
    for low in range(half):
        pair = []
        for h in (low, low + half):
            of_head = jnp.concatenate(
                [
                    latent[q, pl.ds(h, seqs, stride=head_count), :]
                    for q in range(latent_dim // LANES)
                ],
                axis=1,
            )
            pair.append(dot(of_head.astype(BF16), value_up[h]))
        heads[y, c, :, low * VHEAD : (low + 1) * VHEAD] = jnp.concatenate(pair, axis=0).astype(
            BF16
        )

    pl.semaphore_wait(barrier, len(peers))

    mine = heads.at[y, c]
    for d in far_ys:
        send(mine, mine, head_send.at[d], head_recv.at[d], to_y(d))
    send(mine, mine, head_core_send.at[0], head_core_recv.at[0], partner)

    for load in small[2:]:
        load.wait()
    gain_row = gain_ref[...].astype(F32)[None, :]
    router_all[c, g] = jnp.zeros(router_all.shape[2:], F32)
    router_all[c, g, :local_experts, :cols] = router_ref[...].astype(F32) * gain_row
    for d in xs:
        send(
            router_all.at[c, g], router_all.at[c, g], router_send.at[d], router_recv.at[d], to_x(d)
        )
    identity = (
        lax.broadcasted_iota(jnp.int32, (cols, cols), 0)
        == lax.broadcasted_iota(jnp.int32, (cols, cols), 1)
    ).astype(F32)
    gain_column = dot_nt(
        identity.astype(BF16), jnp.broadcast_to(gain_row, (LANES, cols)).astype(BF16)
    )
    loads[3].wait()
    for dst, first in ((weights_out, other * 2), (weights.at[c], c * 2)):
        dst[cols:, :] = jnp.zeros((wide_cols - cols, dst.shape[1]), BF16)
        for j in range(2):
            wide[...] = gate_up[first + j].astype(F32)
            for i in range(2):
                part = wide[pl.ds(i, cols, stride=2), :] * gain_column
                start = (2 * j + i) * LANES
                dst[:cols, start : start + LANES] = part.astype(BF16)
        if dst is weights_out:
            send(weights_out, weights.at[c], weight_send, weight_recv, partner)

    lane = lax.broadcasted_iota(jnp.int32, (block, LANES), 1)
    routes = routes_ref[...]
    slot_of = jnp.zeros(routes.shape, jnp.int32)
    for e in range(expert_slot_ref.shape[0]):
        slot_of = jnp.where(routes == e, expert_slot_ref[e], slot_of)
    used = cols - (wide_cols - LANES)
    slots = expert_slot_ref.shape[0]
    by_slot = jnp.zeros((slots, block), F32)
    slot_at = lax.broadcasted_iota(jnp.int32, (slots, block), 0)
    for k in range(routes.shape[0]):
        by_slot = by_slot + (slot_at == slot_of[k : k + 1, :]).astype(F32)
    same = lax.broadcasted_iota(jnp.int32, (block, block), 0) == lax.broadcasted_iota(
        jnp.int32, (block, block), 1
    )
    by_token = dot_nt(same.astype(F32), by_slot)
    place = lax.broadcasted_iota(jnp.int32, (slots, LANES), 1) - used
    place = (place == lax.broadcasted_iota(jnp.int32, (slots, LANES), 0)).astype(F32)
    extra[...] = dot(by_token, place)
    residual[:, wide_cols - LANES :] = jnp.zeros((block, LANES), F32)
    residual[:, :cols] = residual_ref[...].astype(F32)
    proj_out[:, :, wide_cols - LANES :] = jnp.zeros((nz, block, LANES), BF16)

    for d in ys:
        came = heads.at[at_y(-d), c]
        arrived(came, head_recv.at[d])
        send(came, came, head_core_send.at[d], head_core_recv.at[d], partner)
    loads[2].wait()
    for d in [0] + ys:
        arrived(heads.at[at_y(-d), other], head_core_recv.at[d])

    gathered = heads[...].reshape(ny * 2 * 2 * seqs, half * VHEAD)
    low_part = dot_nt(gathered, out_proj[:, : half * VHEAD]).reshape(ny * 2, 2, seqs, cols)
    high_part = dot_nt(gathered, out_proj[:, half * VHEAD :]).reshape(ny * 2, 2, seqs, cols)
    attn = (low_part[:, 0] + high_part[:, 1]).reshape(nz, block, cols)
    proj_out[:, :, :cols] = attn.astype(BF16)
    for d in far_zs:
        send(proj_out.at[at_z(d)], proj_in.at[t], proj_send.at[d], proj_recv.at[d], to_z(d))

    for d in xs:
        arrived(router_all.at[c, at_x(d)], router_recv.at[d])
    send(router_all.at[c], router_all.at[c], router_send.at[0], router_recv.at[0], partner)
    arrived(weights.at[other], weight_recv)
    arrived(router_all.at[other], router_recv.at[0])
    pad = router_all.shape[2]
    slot_row = lax.broadcasted_iota(jnp.int32, (slots, nx * pad), 0)
    select = (
        lax.broadcasted_iota(jnp.int32, (slots, nx * pad), 1)
        == (slot_row // local_experts) * pad + lax.rem(slot_row, local_experts)
    ).astype(F32).astype(BF16)
    column = lax.broadcasted_iota(jnp.int32, (slots, wide_cols), 1)
    squares_at = (column == cols + slots) | (column == cols + slots + 1)
    for core in range(2):
        packed = router_all[core].reshape(nx * pad, wide_cols).astype(BF16)
        router_rows[core, :slots] = dot(select, packed).astype(BF16)
        router_rows[core, slots:] = squares_at.astype(F32).astype(BF16)

    total = residual[...] + proj_out[t].astype(F32)
    for d in zs:
        arrived(proj_in.at[at_z(-d)], proj_recv.at[d])
        total = total + proj_in[at_z(-d)].astype(F32)
    total = total.astype(BF16).astype(F32)
    stream[...] = total
    squares = jnp.sum(total * total, axis=1, keepdims=True)
    upper = squares.astype(BF16).astype(F32)
    marks = extra[...]
    marks = jnp.where(lane == used + slots, upper, marks)
    marks = jnp.where(lane == used + slots + 1, squares - upper, marks)
    rows[c, g, t, :, : wide_cols - LANES] = total[:, : wide_cols - LANES].astype(BF16)
    rows[c, g, t, :, wide_cols - LANES :] = (total[:, wide_cols - LANES :] + marks).astype(BF16)

    mine = rows.at[c, g, t]
    for d in zs:
        send(mine, mine, row_z_send.at[d], row_z_recv.at[d], to_z(d))
    for a in (2, 1, 3):
        send(mine, mine, row_x_send.at[a, 0], row_x_recv.at[a], to_x(a))
    for d in zs:
        came = rows.at[c, g, at_z(-d)]
        arrived(came, row_z_recv.at[d])
        for a in (2, 1, 3):
            send(came, came, row_x_send.at[a, d], row_x_recv.at[a], to_x(a))
    def pass_rows(a):
        came = rows.at[c, at_x(a)]
        if a:
            arrived(came, row_x_recv.at[a])
        send(came, came, row_core_send.at[a], row_core_recv.at[a], partner)

    def multiply_rows(a):
        of = at_x(a)
        part = dot(rows[c, of].reshape(nz * block, wide_cols), weights[c])
        arrived(rows.at[other, of], row_core_recv.at[a])
        part = part + dot(rows[other, of].reshape(nz * block, wide_cols), weights[other])
        part_out[of] = part.astype(BF16).reshape(nz, block, part.shape[1])
        of_half, place = [(0, 0), (1, 0), (0, 1), (1, 1)][a]
        for d in far_ys:
            send(
                part_out.at[of, at_y(d)],
                part_in.at[of_half, y, place],
                part_send.at[d, a],
                part_recv.at[of_half, d],
                to_y(d),
            )

    chunk = 2 * block
    halves = ((0, 2), (1, 3))
    per_tile = LANES // chunk

    def send_tail(h):
        missing = max(LANES - nz * chunk, 0)
        tail = jnp.zeros((2 * slots, nz * chunk + missing), F32)
        for core in range(2):
            by_owner = jnp.concatenate(
                [
                    rows[core, at_x(code)].reshape(nz, 1, block, wide_cols)
                    for code in halves[h]
                ],
                axis=1,
            ).reshape(nz * chunk, wide_cols)
            if missing:
                by_owner = jnp.concatenate([by_owner, jnp.zeros((missing, wide_cols), BF16)])
            tail = tail + dot_nt(router_rows[core], by_owner)
        lane_of = lax.broadcasted_iota(jnp.int32, (slots, LANES), 1)
        for q in range(ny):
            tile = slice(q // per_tile * LANES, (q // per_tile + 1) * LANES)
            turn = LANES - q % per_tile * chunk
            logits = pltpu.roll(tail[:slots, tile], turn % LANES, 1)
            sums = pltpu.roll(tail[slots:, tile], (turn + chunk) % LANES, 1)
            tail_out[h, q] = jnp.where(lane_of < chunk, logits, sums).astype(BF16)
        for d in far_ys:
            send(
                tail_out.at[h, at_y(d)],
                tail_in.at[h, y],
                tail_send.at[h, d],
                tail_recv.at[h, d],
                to_y(d),
            )

    pass_rows(0)
    multiply_rows(0)
    pass_rows(2)
    pass_rows(1)
    multiply_rows(2)
    send_tail(0)
    pass_rows(3)
    multiply_rows(1)
    multiply_rows(3)
    send_tail(1)

    down_at = lax.broadcasted_iota(jnp.int32, (chunk, LANES), 0)
    across = lax.broadcasted_iota(jnp.int32, (chunk, LANES), 1)
    slot_at = lax.broadcasted_iota(jnp.int32, (chunk, slots), 1)

    def find_hidden(h):
        tail = tail_out[h, y].astype(F32)
        total = jnp.concatenate([part_out[at_x(code), y] for code in halves[h]]).astype(F32)
        for d in ys:
            of = at_y(-d)
            arrived(tail_in.at[h, of], tail_recv.at[h, d])
            tail = tail + tail_in[h, of].astype(F32)
        for d in ys:
            of = at_y(-d)
            arrived(part_in.at[h, of], part_recv.at[h, d])
            total = total + part_in[h, of].reshape(total.shape).astype(F32)
        logits = dot_nt((across == down_at).astype(F32), tail, lax.Precision.HIGHEST)
        sums = dot_nt((across == down_at + chunk).astype(F32), tail, lax.Precision.HIGHEST)
        inv_rms = lax.rsqrt(sums / width + EPSILON)
        marks = jnp.concatenate(
            [rows[c, at_x(code), y, :, wide_cols - LANES :] for code in halves[h]]
        ).astype(F32)
        marks = pltpu.roll(marks, LANES - used, 1)[:, :slots]
        scores = jax.nn.sigmoid(logits * inv_rms) * marks
        shares = scores / jnp.sum(scores, axis=1, keepdims=True)
        inv_rms = inv_rms[:, :1]
        for j in range(2):
            chosen = slot_at == g * local_experts + c * 2 + j
            share = jnp.sum(jnp.where(chosen, shares, 0.0), axis=1, keepdims=True)
            gate = total[:, 2 * j * LANES : (2 * j + 1) * LANES] * inv_rms
            up = total[:, (2 * j + 1) * LANES : (2 * j + 2) * LANES] * inv_rms
            value = jax.nn.silu(gate) * up * share
            hidden[h, c, y, :, j * LANES : (j + 1) * LANES] = value.astype(BF16)
        mine = hidden.at[h, c, y]
        for d in ys:
            send(mine, mine, hid_send.at[h, d], hid_recv.at[h, d], to_y(d))
        send(mine, mine, hid_core_send.at[h, 0], hid_core_recv.at[h, 0], partner)

    down_out[:, :, :, :, wide_cols - LANES :] = jnp.zeros(down_out.shape[:4] + (LANES,), BF16)
    find_hidden(0)
    find_hidden(1)
    for load in loads[4:]:
        load.wait()
    split = down.shape[1] // 2

    def pass_hidden(h, d):
        if d:
            came = hidden.at[h, c, at_y(-d)]
            arrived(came, hid_recv.at[h, d])
            send(came, came, hid_core_send.at[h, d], hid_core_recv.at[h, d], partner)

    def multiply_hidden(h, group):
        for d in group:
            arrived(hidden.at[h, other, at_y(-d)], hid_core_recv.at[h, d])
        low_part = jnp.concatenate([hidden[h, 0, at_y(-d)] for d in group])
        high_part = jnp.concatenate([hidden[h, 1, at_y(-d)] for d in group])
        part = dot_nt(low_part, down[:, :split]) + dot_nt(high_part, down[:, split:])
        part = part.astype(BF16).reshape(len(group), 2, block, cols)
        for i, d in enumerate(group):
            of = at_y(-d)
            down_out[h, of, :, :, :cols] = part[i]
            for place, code in enumerate(halves[h]):
                if code:
                    send(
                        down_out.at[h, of, place],
                        down_in.at[code, of],
                        down_send.at[code, d],
                        down_recv.at[code, d],
                        to_x(code),
                    )

    def to_owner(d):
        return pltpu.make_async_remote_copy(
            src_ref=sum_out.at[at_y(-d)],
            dst_ref=sum_in.at[t],
            send_sem=sum_send.at[d],
            recv_sem=sum_recv.at[t],
            device_id=(g, dp, at_y(-d)),
            device_id_type=MESH,
        )

    def add_groups(d):
        of = at_y(-d)
        total = down_out[0, of, 0].astype(F32)
        for a in (2, 1, 3):
            arrived(down_in.at[a, of], down_recv.at[a, d])
            total = total + down_in[a, of].astype(F32)
        sum_out[of] = total.astype(BF16)

        @pl.when(of != t)
        def _():
            to_owner(d).start()

    order = [0] + ys
    first = [order[i : i + 4] for i in range(0, ny, 4)]
    second = [order[i : i + 2] for i in range(0, ny, 2)]
    steps = [(0, group) for group in first] + [(1, group) for group in second]
    for d in steps[0][1]:
        pass_hidden(0, d)
    for i, (h, group) in enumerate(steps):
        if i + 1 < len(steps):
            for d in steps[i + 1][1]:
                pass_hidden(steps[i + 1][0], d)
        multiply_hidden(h, group)
        if i - len(first) >= 2:
            for d in second[i - len(first) - 2]:
                add_groups(d)
    for group in second[-2:]:
        for d in group:
            add_groups(d)
    total = stream[...] + sum_out[t].astype(F32)
    for d in zs:
        of = at_z(-d)
        arrived(sum_in.at[of], sum_recv.at[of])
        total = total + sum_in[of].astype(F32)
    out_ref[...] = total[:, :cols].astype(BF16)

    for d in order:

        @pl.when(at_y(-d) != t)
        def _():
            to_owner(d).wait_send()

    for copy in sent:
        copy.wait_send()


def on_device(sizes, width, *arrays):
    (
        queries,
        latent_cache,
        lengths,
        value_up,
        out_proj,
        residual_in,
        norm_gain,
        router,
        gate_up,
        down_proj,
        routes,
        expert_slot,
    ) = arrays
    nx, ny, nz = sizes
    seqs, head_count, depth = queries.shape
    block, cols = residual_in.shape
    experts, _, _, units = gate_up.shape
    gate_up = gate_up.reshape(experts, cols * 2, units)
    down_proj = jnp.swapaxes(down_proj, 1, 2)
    latent_cache = jnp.swapaxes(latent_cache, 1, 2)
    out_proj = out_proj.T
    routes = routes.T
    wide_cols = -(-cols // LANES) * LANES
    latent_dim = value_up.shape[1]
    slots = expert_slot.shape[0]
    vmem = pl.BlockSpec(memory_space=pltpu.VMEM)
    anywhere = pl.BlockSpec(memory_space=pltpu.HBM)
    sem = pltpu.SemaphoreType.DMA
    scratch = [
        pltpu.SMEM(lengths.shape, jnp.int32),
        pltpu.SMEM(expert_slot.shape, jnp.int32),
        pltpu.VMEM(queries.shape, BF16),
        pltpu.VMEM(residual_in.shape, BF16),
        pltpu.VMEM(norm_gain.shape, BF16),
        pltpu.VMEM(router.shape, BF16),
        pltpu.VMEM(routes.shape, jnp.int32),
        pltpu.VMEM(latent_cache.shape, BF16),
        pltpu.VMEM(value_up.shape, BF16),
        pltpu.VMEM(out_proj.shape, BF16),
        pltpu.VMEM(gate_up.shape, BF16),
        pltpu.VMEM((cols, experts * units), BF16),
        pltpu.VMEM((latent_dim // LANES, seqs * head_count, LANES), F32),
        pltpu.VMEM((ny, 2, 2 * seqs, head_count // 2 * VHEAD), BF16),
        pltpu.VMEM((nz, block, wide_cols), BF16),
        pltpu.VMEM((nz, block, wide_cols), BF16),
        pltpu.VMEM((block, wide_cols), F32),
        pltpu.VMEM((block, LANES), F32),
        pltpu.VMEM((block, wide_cols), F32),
        pltpu.VMEM((2, nx, nz, block, wide_cols), BF16),
        pltpu.VMEM((cols * 2, units), F32),
        pltpu.VMEM((2, wide_cols, 4 * units), BF16),
        pltpu.VMEM((wide_cols, 4 * units), BF16),
        pltpu.VMEM((2, nx, 8, wide_cols), F32),
        pltpu.VMEM((2, 2 * slots, wide_cols), BF16),
        pltpu.VMEM((nx, nz, block, 4 * units), BF16),
        pltpu.VMEM((2, ny, 2, block, 4 * units), BF16),
        pltpu.VMEM((2, ny, slots, LANES), BF16),
        pltpu.VMEM((2, ny, slots, LANES), BF16),
        pltpu.VMEM((2, 2, ny, 2 * block, 2 * units), BF16),
        pltpu.VMEM((2, ny, 2, block, wide_cols), BF16),
        pltpu.VMEM((nx, ny, block, wide_cols), BF16),
        pltpu.VMEM((nz, block, wide_cols), BF16),
        pltpu.VMEM((nz, block, wide_cols), BF16),
        sem((4 + experts,)),
        sem((7,)),
        sem((ny,)),
        sem((ny,)),
        sem((ny,)),
        sem((ny,)),
        sem,
        sem,
        sem((nx,)),
        sem((nx,)),
        sem((nz,)),
        sem((nz,)),
        sem((nz,)),
        sem((nz,)),
        sem((nx, nz)),
        sem((nx,)),
        sem((nx,)),
        sem((nx,)),
        sem((ny, nx)),
        sem((2, ny)),
        sem((2, ny)),
        sem((2, ny)),
        sem((2, ny)),
        sem((2, ny)),
        sem((2, ny)),
        sem((2, ny)),
        sem((nx, ny)),
        sem((nx, ny)),
        sem((nz,)),
        sem((nz,)),
    ]
    return pl.pallas_call(
        functools.partial(kernel, sizes, width),
        out_shape=jax.ShapeDtypeStruct((block, cols), BF16),
        in_specs=[anywhere] * 12,
        out_specs=vmem,
        scratch_shapes=scratch,
        name="decode_layer",
        compiler_params=pltpu.CompilerParams(
            collective_id=0, has_side_effects=True, vmem_limit_bytes=60 * 2**20
        ),
    )(
        lengths,
        expert_slot,
        queries,
        residual_in,
        norm_gain,
        router,
        routes,
        latent_cache,
        value_up,
        out_proj,
        gate_up,
        down_proj,
    )


def solution(mesh):
    in_specs = (
        P(("grp", "dp"), "tensor", None),
        P(("grp", "dp"), None, None),
        P(("grp", "dp")),
        P("tensor", None, None),
        P("tensor", "dp"),
        P(("grp", "tensor"), "dp"),
        P("dp"),
        P("grp", "dp"),
        P("grp", "dp", None, "tensor"),
        P("grp", "tensor", "dp"),
        P(("grp", "tensor"), None),
        P(),
    )
    out_specs = P(("grp", "tensor"), "dp")
    sizes = (mesh.shape["grp"], mesh.shape["dp"] // 2, mesh.shape["tensor"])

    def whole(*arrays):
        width = arrays[5].shape[1]
        return jax.shard_map(
            functools.partial(on_device, sizes, width),
            mesh=mesh,
            in_specs=in_specs,
            out_specs=out_specs,
            check_vma=False,
        )(*arrays)

    return whole
```

```python
import functools

import jax
import jax.numpy as jnp
from jax import lax
from jax.experimental import pallas as pl
from jax.experimental.pallas import tpu as pltpu
from jax.sharding import PartitionSpec as P

ROPE = 64
VHEAD = 128
EPSILON = 1e-06
MESH = pl.DeviceIdType.MESH
BF16 = jnp.bfloat16
F32 = jnp.float32
LANES = 128


def dot(a, b):
    return jnp.dot(a, b, preferred_element_type=F32)


def dot_nt(a, b, precision=None):
    return lax.dot_general(
        a, b, (((1,), (1,)), ((), ())), preferred_element_type=F32, precision=precision
    )


def near_first(count):
    return sorted(range(1, count), key=lambda d: (min(d, count - d), d))


def kernel(
    sizes,
    width,
    lengths_hbm,
    expert_slot_hbm,
    queries_hbm,
    residual_hbm,
    gain_hbm,
    router_hbm,
    routes_hbm,
    cache_hbm,
    value_up_hbm,
    out_proj_hbm,
    gate_up_hbm,
    down_hbm,
    out_ref,
    lengths_ref,
    expert_slot_ref,
    queries_ref,
    residual_ref,
    gain_ref,
    router_ref,
    routes_ref,
    cache,
    value_up,
    out_proj,
    gate_up,
    down,
    latent,
    heads,
    proj_out,
    proj_in,
    residual,
    extra,
    stream,
    rows,
    wide,
    weights,
    weights_out,
    router_all,
    router_rows,
    part_out,
    part_in,
    tail_out,
    tail_in,
    hidden,
    down_out,
    down_in,
    sum_out,
    sum_in,
    load_sem,
    cache_sem,
    small_sem,
    head_send,
    head_recv,
    head_core_send,
    head_core_recv,
    weight_send,
    weight_recv,
    router_send,
    router_recv,
    proj_send,
    proj_recv,
    row_z_send,
    row_z_recv,
    row_x_send,
    row_x_recv,
    row_core_send,
    row_core_recv,
    part_send,
    part_recv,
    tail_send,
    tail_recv,
    hid_send,
    hid_recv,
    hid_core_send,
    hid_core_recv,
    down_send,
    down_recv,
    sum_send,
    sum_recv,
):
    nx, ny, nz = sizes
    g = lax.axis_index("grp")
    dp = lax.axis_index("dp")
    t = lax.axis_index("tensor")
    y = dp // 2
    c = lax.rem(dp, 2)
    other = 1 - c
    cols = residual_ref.shape[1]
    block = residual_ref.shape[0]
    wide_cols = stream.shape[1]
    seqs, head_count, depth = queries_ref.shape
    latent_dim = value_up.shape[1]
    local_experts = router_ref.shape[0]
    ys, zs = near_first(ny), near_first(nz)
    xs = [1, 3, 2]
    far_ys, far_zs = ys[::-1], zs[::-1]

    def at_x(code):
        return [g, g + 1 - 2 * lax.rem(g, 2), lax.rem(g + 2, nx), nx - 1 - g][code]

    def at_y(d):
        return lax.rem(y + ny + d, ny)

    def at_z(d):
        return lax.rem(t + nz + d, nz)

    def to_x(d):
        return (at_x(d), dp, t)

    def to_y(d):
        return (g, at_y(d) * 2 + c, t)

    def to_z(d):
        return (g, dp, at_z(d))

    partner = (g, y * 2 + other, t)
    sent = []

    def send(src, dst, send_sem, recv_sem, device):
        copy = pltpu.make_async_remote_copy(
            src_ref=src,
            dst_ref=dst,
            send_sem=send_sem,
            recv_sem=recv_sem,
            device_id=device,
            device_id_type=MESH,
        )
        copy.start()
        sent.append(copy)

    def arrived(dst, recv_sem):
        pltpu.make_async_remote_copy(
            src_ref=dst,
            dst_ref=dst,
            send_sem=load_sem.at[0],
            recv_sem=recv_sem,
            device_id=partner,
            device_id_type=MESH,
        ).wait_recv()

    small = [
        pltpu.make_async_copy(src, dst, small_sem.at[i])
        for i, (src, dst) in enumerate(
            [
                (lengths_hbm, lengths_ref),
                (queries_hbm, queries_ref),
                (expert_slot_hbm, expert_slot_ref),
                (gain_hbm, gain_ref),
                (router_hbm, router_ref),
                (routes_hbm, routes_ref),
                (residual_hbm, residual_ref),
            ]
        )
    ]

    loads = [
        pltpu.make_async_copy(src, dst, load_sem.at[i])
        for i, (src, dst) in enumerate(
            [
                (value_up_hbm, value_up),
                (out_proj_hbm, out_proj),
                (gate_up_hbm, gate_up),
            ]
            + [
                (down_hbm.at[e], down.at[:, pl.ds(e * down_hbm.shape[2], down_hbm.shape[2])])
                for e in range(local_experts)
            ]
        )
    ]
    cached = [
        pltpu.make_async_copy(cache_hbm.at[n], cache.at[n], cache_sem.at[n]) for n in range(seqs)
    ]
    for load in small[:2] + cached + loads[:1]:
        load.start()

    barrier = pltpu.get_barrier_semaphore()
    peers = [partner] + [to_y(d) for d in ys] + [to_z(d) for d in zs] + [to_x(d) for d in xs]
    for device in peers:
        pl.semaphore_signal(barrier, inc=1, device_id=device, device_id_type=MESH)

    score_scale = (VHEAD + ROPE) ** (-0.5)
    for load in small[:2] + cached:
        load.wait()
    scores = []
    positions = lax.broadcasted_iota(jnp.int32, (head_count, cache.shape[2]), 1)
    for n in range(seqs):
        of_seq = dot(queries_ref[n], cache[n]) * score_scale
        scores.append(jnp.where(positions < lengths_ref[n], of_seq, -1e30))
    for load in small[2:] + loads[1:]:
        load.start()
    scores = jnp.concatenate(scores)
    exps = jnp.exp(scores - jnp.max(scores, axis=1, keepdims=True))
    probs = exps / jnp.sum(exps, axis=1, keepdims=True)
    for n in range(seqs):
        of_heads = slice(n * head_count, (n + 1) * head_count)
        of_seq = dot_nt(probs[of_heads].astype(BF16), cache[n, :latent_dim, :])
        for q in range(latent_dim // LANES):
            latent[q, of_heads, :] = of_seq[:, q * LANES : (q + 1) * LANES]
    loads[0].wait()
    half = head_count // 2
    for low in range(half):
        pair = []
        for h in (low, low + half):
            of_head = jnp.concatenate(
                [
                    latent[q, pl.ds(h, seqs, stride=head_count), :]
                    for q in range(latent_dim // LANES)
                ],
                axis=1,
            )
            pair.append(dot(of_head.astype(BF16), value_up[h]))
        heads[y, c, :, low * VHEAD : (low + 1) * VHEAD] = jnp.concatenate(pair, axis=0).astype(
            BF16
        )

    pl.semaphore_wait(barrier, len(peers))

    mine = heads.at[y, c]
    for d in far_ys:
        send(mine, mine, head_send.at[d], head_recv.at[d], to_y(d))
    send(mine, mine, head_core_send.at[0], head_core_recv.at[0], partner)

    for load in small[2:]:
        load.wait()
    gain_row = gain_ref[...].astype(F32)[None, :]
    router_all[c, g] = jnp.zeros(router_all.shape[2:], F32)
    router_all[c, g, :local_experts, :cols] = router_ref[...].astype(F32) * gain_row
    for d in xs:
        send(
            router_all.at[c, g], router_all.at[c, g], router_send.at[d], router_recv.at[d], to_x(d)
        )
    identity = (
        lax.broadcasted_iota(jnp.int32, (cols, cols), 0)
        == lax.broadcasted_iota(jnp.int32, (cols, cols), 1)
    ).astype(F32)
    gain_column = dot_nt(
        identity.astype(BF16), jnp.broadcast_to(gain_row, (LANES, cols)).astype(BF16)
    )
    loads[2].wait()
    for dst, first in ((weights_out, other * 2), (weights.at[c], c * 2)):
        dst[cols:, :] = jnp.zeros((wide_cols - cols, dst.shape[1]), BF16)
        for j in range(2):
            wide[...] = gate_up[first + j].astype(F32)
            for i in range(2):
                part = wide[pl.ds(i, cols, stride=2), :] * gain_column
                start = (2 * j + i) * LANES
                dst[:cols, start : start + LANES] = part.astype(BF16)
        if dst is weights_out:
            send(weights_out, weights.at[c], weight_send, weight_recv, partner)

    lane = lax.broadcasted_iota(jnp.int32, (block, LANES), 1)
    routes = routes_ref[...]
    slot_of = jnp.zeros(routes.shape, jnp.int32)
    for e in range(expert_slot_ref.shape[0]):
        slot_of = jnp.where(routes == e, expert_slot_ref[e], slot_of)
    used = cols - (wide_cols - LANES)
    slots = expert_slot_ref.shape[0]
    by_slot = jnp.zeros((slots, block), F32)
    slot_at = lax.broadcasted_iota(jnp.int32, (slots, block), 0)
    for k in range(routes.shape[0]):
        by_slot = by_slot + (slot_at == slot_of[k : k + 1, :]).astype(F32)
    same = lax.broadcasted_iota(jnp.int32, (block, block), 0) == lax.broadcasted_iota(
        jnp.int32, (block, block), 1
    )
    by_token = dot_nt(same.astype(F32), by_slot)
    place = lax.broadcasted_iota(jnp.int32, (slots, LANES), 1) - used
    place = (place == lax.broadcasted_iota(jnp.int32, (slots, LANES), 0)).astype(F32)
    extra[...] = dot(by_token, place)
    residual[:, wide_cols - LANES :] = jnp.zeros((block, LANES), F32)
    residual[:, :cols] = residual_ref[...].astype(F32)
    proj_out[:, :, wide_cols - LANES :] = jnp.zeros((nz, block, LANES), BF16)

    for d in ys:
        came = heads.at[at_y(-d), c]
        arrived(came, head_recv.at[d])
        send(came, came, head_core_send.at[d], head_core_recv.at[d], partner)
    loads[1].wait()
    for d in [0] + ys:
        arrived(heads.at[at_y(-d), other], head_core_recv.at[d])

    gathered = heads[...].reshape(ny * 2 * 2 * seqs, half * VHEAD)
    low_part = dot_nt(gathered, out_proj[:, : half * VHEAD]).reshape(ny * 2, 2, seqs, cols)
    high_part = dot_nt(gathered, out_proj[:, half * VHEAD :]).reshape(ny * 2, 2, seqs, cols)
    attn = (low_part[:, 0] + high_part[:, 1]).reshape(nz, block, cols)
    proj_out[:, :, :cols] = attn.astype(BF16)
    for d in far_zs:
        send(proj_out.at[at_z(d)], proj_in.at[t], proj_send.at[d], proj_recv.at[d], to_z(d))

    for d in xs:
        arrived(router_all.at[c, at_x(d)], router_recv.at[d])
    send(router_all.at[c], router_all.at[c], router_send.at[0], router_recv.at[0], partner)
    arrived(weights.at[other], weight_recv)
    arrived(router_all.at[other], router_recv.at[0])
    pad = router_all.shape[2]
    slot_row = lax.broadcasted_iota(jnp.int32, (slots, nx * pad), 0)
    select = (
        lax.broadcasted_iota(jnp.int32, (slots, nx * pad), 1)
        == (slot_row // local_experts) * pad + lax.rem(slot_row, local_experts)
    ).astype(F32).astype(BF16)
    column = lax.broadcasted_iota(jnp.int32, (slots, wide_cols), 1)
    squares_at = (column == cols + slots) | (column == cols + slots + 1)
    for core in range(2):
        packed = router_all[core].reshape(nx * pad, wide_cols).astype(BF16)
        router_rows[core, :slots] = dot(select, packed).astype(BF16)
        router_rows[core, slots:] = squares_at.astype(F32).astype(BF16)

    total = residual[...] + proj_out[t].astype(F32)
    for d in zs:
        arrived(proj_in.at[at_z(-d)], proj_recv.at[d])
        total = total + proj_in[at_z(-d)].astype(F32)
    total = total.astype(BF16).astype(F32)
    stream[...] = total
    squares = jnp.sum(total * total, axis=1, keepdims=True)
    upper = squares.astype(BF16).astype(F32)
    marks = extra[...]
    marks = jnp.where(lane == used + slots, upper, marks)
    marks = jnp.where(lane == used + slots + 1, squares - upper, marks)
    rows[c, g, t, :, : wide_cols - LANES] = total[:, : wide_cols - LANES].astype(BF16)
    rows[c, g, t, :, wide_cols - LANES :] = (total[:, wide_cols - LANES :] + marks).astype(BF16)

    mine = rows.at[c, g, t]
    for d in zs:
        send(mine, mine, row_z_send.at[d], row_z_recv.at[d], to_z(d))
    for a in (2, 1, 3):
        send(mine, mine, row_x_send.at[a, 0], row_x_recv.at[a], to_x(a))
    for d in zs:
        came = rows.at[c, g, at_z(-d)]
        arrived(came, row_z_recv.at[d])
        for a in (2, 1, 3):
            send(came, came, row_x_send.at[a, d], row_x_recv.at[a], to_x(a))
    def pass_rows(a):
        came = rows.at[c, at_x(a)]
        if a:
            arrived(came, row_x_recv.at[a])
        send(came, came, row_core_send.at[a], row_core_recv.at[a], partner)

    def multiply_rows(a):
        of = at_x(a)
        part = dot(rows[c, of].reshape(nz * block, wide_cols), weights[c])
        arrived(rows.at[other, of], row_core_recv.at[a])
        part = part + dot(rows[other, of].reshape(nz * block, wide_cols), weights[other])
        part_out[of] = part.astype(BF16).reshape(nz, block, part.shape[1])
        of_half, place = [(0, 0), (1, 0), (0, 1), (1, 1)][a]
        for d in far_ys:
            send(
                part_out.at[of, at_y(d)],
                part_in.at[of_half, y, place],
                part_send.at[d, a],
                part_recv.at[of_half, d],
                to_y(d),
            )

    chunk = 2 * block
    halves = ((0, 2), (1, 3))
    per_tile = LANES // chunk

    def send_tail(h):
        missing = max(LANES - nz * chunk, 0)
        tail = jnp.zeros((2 * slots, nz * chunk + missing), F32)
        for core in range(2):
            by_owner = jnp.concatenate(
                [
                    rows[core, at_x(code)].reshape(nz, 1, block, wide_cols)
                    for code in halves[h]
                ],
                axis=1,
            ).reshape(nz * chunk, wide_cols)
            if missing:
                by_owner = jnp.concatenate([by_owner, jnp.zeros((missing, wide_cols), BF16)])
            tail = tail + dot_nt(router_rows[core], by_owner)
        lane_of = lax.broadcasted_iota(jnp.int32, (slots, LANES), 1)
        for q in range(ny):
            tile = slice(q // per_tile * LANES, (q // per_tile + 1) * LANES)
            turn = LANES - q % per_tile * chunk
            logits = pltpu.roll(tail[:slots, tile], turn % LANES, 1)
            sums = pltpu.roll(tail[slots:, tile], (turn + chunk) % LANES, 1)
            tail_out[h, q] = jnp.where(lane_of < chunk, logits, sums).astype(BF16)
        for d in far_ys:
            send(
                tail_out.at[h, at_y(d)],
                tail_in.at[h, y],
                tail_send.at[h, d],
                tail_recv.at[h, d],
                to_y(d),
            )

    pass_rows(0)
    multiply_rows(0)
    pass_rows(2)
    pass_rows(1)
    multiply_rows(2)
    send_tail(0)
    pass_rows(3)
    multiply_rows(1)
    multiply_rows(3)
    send_tail(1)

    down_at = lax.broadcasted_iota(jnp.int32, (chunk, LANES), 0)
    across = lax.broadcasted_iota(jnp.int32, (chunk, LANES), 1)
    slot_at = lax.broadcasted_iota(jnp.int32, (chunk, slots), 1)

    def find_hidden(h):
        tail = tail_out[h, y].astype(F32)
        total = jnp.concatenate([part_out[at_x(code), y] for code in halves[h]]).astype(F32)
        for d in ys:
            of = at_y(-d)
            arrived(tail_in.at[h, of], tail_recv.at[h, d])
            tail = tail + tail_in[h, of].astype(F32)
        for d in ys:
            of = at_y(-d)
            arrived(part_in.at[h, of], part_recv.at[h, d])
            total = total + part_in[h, of].reshape(total.shape).astype(F32)
        logits = dot_nt((across == down_at).astype(F32), tail, lax.Precision.HIGHEST)
        sums = dot_nt((across == down_at + chunk).astype(F32), tail, lax.Precision.HIGHEST)
        inv_rms = lax.rsqrt(sums / width + EPSILON)
        marks = jnp.concatenate(
            [rows[c, at_x(code), y, :, wide_cols - LANES :] for code in halves[h]]
        ).astype(F32)
        marks = pltpu.roll(marks, LANES - used, 1)[:, :slots]
        scores = jax.nn.sigmoid(logits * inv_rms) * marks
        shares = scores / jnp.sum(scores, axis=1, keepdims=True)
        inv_rms = inv_rms[:, :1]
        for j in range(2):
            chosen = slot_at == g * local_experts + c * 2 + j
            share = jnp.sum(jnp.where(chosen, shares, 0.0), axis=1, keepdims=True)
            gate = total[:, 2 * j * LANES : (2 * j + 1) * LANES] * inv_rms
            up = total[:, (2 * j + 1) * LANES : (2 * j + 2) * LANES] * inv_rms
            value = jax.nn.silu(gate) * up * share
            hidden[h, c, y, :, j * LANES : (j + 1) * LANES] = value.astype(BF16)
        mine = hidden.at[h, c, y]
        for d in ys:
            send(mine, mine, hid_send.at[h, d], hid_recv.at[h, d], to_y(d))
        send(mine, mine, hid_core_send.at[h, 0], hid_core_recv.at[h, 0], partner)

    down_out[:, :, :, :, wide_cols - LANES :] = jnp.zeros(down_out.shape[:4] + (LANES,), BF16)
    find_hidden(0)
    find_hidden(1)
    for load in loads[3:]:
        load.wait()
    split = down.shape[1] // 2

    def pass_hidden(h, d):
        if d:
            came = hidden.at[h, c, at_y(-d)]
            arrived(came, hid_recv.at[h, d])
            send(came, came, hid_core_send.at[h, d], hid_core_recv.at[h, d], partner)

    def multiply_hidden(h, group):
        for d in group:
            arrived(hidden.at[h, other, at_y(-d)], hid_core_recv.at[h, d])
        low_part = jnp.concatenate([hidden[h, 0, at_y(-d)] for d in group])
        high_part = jnp.concatenate([hidden[h, 1, at_y(-d)] for d in group])
        part = dot_nt(low_part, down[:, :split]) + dot_nt(high_part, down[:, split:])
        part = part.astype(BF16).reshape(len(group), 2, block, cols)
        for i, d in enumerate(group):
            of = at_y(-d)
            down_out[h, of, :, :, :cols] = part[i]
            for place, code in enumerate(halves[h]):
                if code:
                    send(
                        down_out.at[h, of, place],
                        down_in.at[code, of],
                        down_send.at[code, d],
                        down_recv.at[code, d],
                        to_x(code),
                    )

    def to_owner(d):
        return pltpu.make_async_remote_copy(
            src_ref=sum_out.at[at_y(-d)],
            dst_ref=sum_in.at[t],
            send_sem=sum_send.at[d],
            recv_sem=sum_recv.at[t],
            device_id=(g, dp, at_y(-d)),
            device_id_type=MESH,
        )

    def add_groups(d):
        of = at_y(-d)
        total = down_out[0, of, 0].astype(F32)
        for a in (2, 1, 3):
            arrived(down_in.at[a, of], down_recv.at[a, d])
            total = total + down_in[a, of].astype(F32)
        sum_out[of] = total.astype(BF16)

        @pl.when(of != t)
        def _():
            to_owner(d).start()

    order = [0] + ys
    first = [order[i : i + 4] for i in range(0, ny, 4)]
    second = [order[i : i + 2] for i in range(0, ny, 2)]
    steps = [(0, group) for group in first] + [(1, group) for group in second]
    for d in steps[0][1]:
        pass_hidden(0, d)
    for i, (h, group) in enumerate(steps):
        if i + 1 < len(steps):
            for d in steps[i + 1][1]:
                pass_hidden(steps[i + 1][0], d)
        multiply_hidden(h, group)
        if i - len(first) >= 2:
            for d in second[i - len(first) - 2]:
                add_groups(d)
    for group in second[-2:]:
        for d in group:
            add_groups(d)
    total = stream[...] + sum_out[t].astype(F32)
    for d in zs:
        of = at_z(-d)
        arrived(sum_in.at[of], sum_recv.at[of])
        total = total + sum_in[of].astype(F32)
    out_ref[...] = total[:, :cols].astype(BF16)

    for d in order:

        @pl.when(at_y(-d) != t)
        def _():
            to_owner(d).wait_send()

    for copy in sent:
        copy.wait_send()


def on_device(sizes, width, *arrays):
    (
        queries,
        latent_cache,
        lengths,
        value_up,
        out_proj,
        residual_in,
        norm_gain,
        router,
        gate_up,
        down_proj,
        routes,
        expert_slot,
    ) = arrays
    nx, ny, nz = sizes
    seqs, head_count, depth = queries.shape
    block, cols = residual_in.shape
    experts, _, _, units = gate_up.shape
    gate_up = gate_up.reshape(experts, cols * 2, units)
    down_proj = jnp.swapaxes(down_proj, 1, 2)
    latent_cache = jnp.swapaxes(latent_cache, 1, 2)
    out_proj = out_proj.T
    routes = routes.T
    wide_cols = -(-cols // LANES) * LANES
    latent_dim = value_up.shape[1]
    slots = expert_slot.shape[0]
    vmem = pl.BlockSpec(memory_space=pltpu.VMEM)
    anywhere = pl.BlockSpec(memory_space=pltpu.HBM)
    sem = pltpu.SemaphoreType.DMA
    scratch = [
        pltpu.SMEM(lengths.shape, jnp.int32),
        pltpu.SMEM(expert_slot.shape, jnp.int32),
        pltpu.VMEM(queries.shape, BF16),
        pltpu.VMEM(residual_in.shape, BF16),
        pltpu.VMEM(norm_gain.shape, BF16),
        pltpu.VMEM(router.shape, BF16),
        pltpu.VMEM(routes.shape, jnp.int32),
        pltpu.VMEM(latent_cache.shape, BF16),
        pltpu.VMEM(value_up.shape, BF16),
        pltpu.VMEM(out_proj.shape, BF16),
        pltpu.VMEM(gate_up.shape, BF16),
        pltpu.VMEM((cols, experts * units), BF16),
        pltpu.VMEM((latent_dim // LANES, seqs * head_count, LANES), F32),
        pltpu.VMEM((ny, 2, 2 * seqs, head_count // 2 * VHEAD), BF16),
        pltpu.VMEM((nz, block, wide_cols), BF16),
        pltpu.VMEM((nz, block, wide_cols), BF16),
        pltpu.VMEM((block, wide_cols), F32),
        pltpu.VMEM((block, LANES), F32),
        pltpu.VMEM((block, wide_cols), F32),
        pltpu.VMEM((2, nx, nz, block, wide_cols), BF16),
        pltpu.VMEM((cols * 2, units), F32),
        pltpu.VMEM((2, wide_cols, 4 * units), BF16),
        pltpu.VMEM((wide_cols, 4 * units), BF16),
        pltpu.VMEM((2, nx, 8, wide_cols), F32),
        pltpu.VMEM((2, 2 * slots, wide_cols), BF16),
        pltpu.VMEM((nx, nz, block, 4 * units), BF16),
        pltpu.VMEM((2, ny, 2, block, 4 * units), BF16),
        pltpu.VMEM((2, ny, slots, LANES), BF16),
        pltpu.VMEM((2, ny, slots, LANES), BF16),
        pltpu.VMEM((2, 2, ny, 2 * block, 2 * units), BF16),
        pltpu.VMEM((2, ny, 2, block, wide_cols), BF16),
        pltpu.VMEM((nx, ny, block, wide_cols), BF16),
        pltpu.VMEM((nz, block, wide_cols), BF16),
        pltpu.VMEM((nz, block, wide_cols), BF16),
        sem((3 + experts,)),
        sem((seqs,)),
        sem((7,)),
        sem((ny,)),
        sem((ny,)),
        sem((ny,)),
        sem((ny,)),
        sem,
        sem,
        sem((nx,)),
        sem((nx,)),
        sem((nz,)),
        sem((nz,)),
        sem((nz,)),
        sem((nz,)),
        sem((nx, nz)),
        sem((nx,)),
        sem((nx,)),
        sem((nx,)),
        sem((ny, nx)),
        sem((2, ny)),
        sem((2, ny)),
        sem((2, ny)),
        sem((2, ny)),
        sem((2, ny)),
        sem((2, ny)),
        sem((2, ny)),
        sem((nx, ny)),
        sem((nx, ny)),
        sem((nz,)),
        sem((nz,)),
    ]
    return pl.pallas_call(
        functools.partial(kernel, sizes, width),
        out_shape=pltpu.VMEM((block, cols), BF16),
        in_specs=[anywhere] * 12,
        out_specs=vmem,
        scratch_shapes=scratch,
        name="decode_layer",
        compiler_params=pltpu.CompilerParams(
            collective_id=0, has_side_effects=True, vmem_limit_bytes=60 * 2**20
        ),
    )(
        lengths,
        expert_slot,
        queries,
        residual_in,
        norm_gain,
        router,
        routes,
        latent_cache,
        value_up,
        out_proj,
        gate_up,
        down_proj,
    )


def solution(mesh):
    in_specs = (
        P(("grp", "dp"), "tensor", None),
        P(("grp", "dp"), None, None),
        P(("grp", "dp")),
        P("tensor", None, None),
        P("tensor", "dp"),
        P(("grp", "tensor"), "dp"),
        P("dp"),
        P("grp", "dp"),
        P("grp", "dp", None, "tensor"),
        P("grp", "tensor", "dp"),
        P(("grp", "tensor"), None),
        P(),
    )
    out_specs = P(("grp", "tensor"), "dp")
    sizes = (mesh.shape["grp"], mesh.shape["dp"] // 2, mesh.shape["tensor"])

    def whole(*arrays):
        width = arrays[5].shape[1]
        return jax.shard_map(
            functools.partial(on_device, sizes, width),
            mesh=mesh,
            in_specs=in_specs,
            out_specs=out_specs,
            check_vma=False,
        )(*arrays)

    return whole
```

```python
import functools

import jax
import jax.numpy as jnp
from jax import lax
from jax.experimental import pallas as pl
from jax.experimental.pallas import tpu as pltpu
from jax.sharding import PartitionSpec as P

ROPE = 64
VHEAD = 128
EPSILON = 1e-06
MESH = pl.DeviceIdType.MESH
BF16 = jnp.bfloat16
F32 = jnp.float32
LANES = 128


def dot(a, b):
    return jnp.dot(a, b, preferred_element_type=F32)


def dot_nt(a, b, precision=None):
    return lax.dot_general(
        a, b, (((1,), (1,)), ((), ())), preferred_element_type=F32, precision=precision
    )


def near_first(count):
    return sorted(range(1, count), key=lambda d: (min(d, count - d), d))


def kernel(
    sizes,
    width,
    lengths_hbm,
    expert_slot_hbm,
    queries_hbm,
    residual_hbm,
    gain_hbm,
    router_hbm,
    routes_hbm,
    cache_hbm,
    value_up_hbm,
    out_proj_hbm,
    gate_up_hbm,
    down_hbm,
    out_ref,
    lengths_ref,
    expert_slot_ref,
    queries_ref,
    residual_ref,
    gain_ref,
    router_ref,
    routes_ref,
    cache,
    value_up,
    out_proj,
    gate_up,
    down,
    latent,
    heads,
    proj_out,
    proj_in,
    residual,
    extra,
    stream,
    rows,
    wide,
    weights,
    weights_out,
    router_all,
    router_rows,
    part_out,
    part_in,
    tail_out,
    tail_in,
    hidden,
    down_out,
    down_in,
    sum_out,
    sum_in,
    load_sem,
    cache_sem,
    small_sem,
    head_send,
    head_recv,
    head_core_send,
    head_core_recv,
    weight_send,
    weight_recv,
    router_send,
    router_recv,
    proj_send,
    proj_recv,
    row_z_send,
    row_z_recv,
    row_x_send,
    row_x_recv,
    row_core_send,
    row_core_recv,
    part_send,
    part_recv,
    tail_send,
    tail_recv,
    hid_send,
    hid_recv,
    hid_core_send,
    hid_core_recv,
    down_send,
    down_recv,
    sum_send,
    sum_recv,
):
    nx, ny, nz = sizes
    g = lax.axis_index("grp")
    dp = lax.axis_index("dp")
    t = lax.axis_index("tensor")
    y = dp // 2
    c = lax.rem(dp, 2)
    other = 1 - c
    cols = residual_ref.shape[1]
    block = residual_ref.shape[0]
    wide_cols = stream.shape[1]
    seqs, head_count, depth = queries_ref.shape
    latent_dim = value_up.shape[1]
    local_experts = router_ref.shape[0]
    ys, zs = near_first(ny), near_first(nz)
    xs = [1, 3, 2]
    far_ys, far_zs = ys[::-1], zs[::-1]

    def at_x(code):
        return [g, g + 1 - 2 * lax.rem(g, 2), lax.rem(g + 2, nx), nx - 1 - g][code]

    def at_y(d):
        return lax.rem(y + ny + d, ny)

    def at_z(d):
        return lax.rem(t + nz + d, nz)

    def to_x(d):
        return (at_x(d), dp, t)

    def to_y(d):
        return (g, at_y(d) * 2 + c, t)

    def to_z(d):
        return (g, dp, at_z(d))

    partner = (g, y * 2 + other, t)

    def send(src, dst, send_sem, recv_sem, device):
        copy = pltpu.make_async_remote_copy(
            src_ref=src,
            dst_ref=dst,
            send_sem=send_sem,
            recv_sem=recv_sem,
            device_id=device,
            device_id_type=MESH,
        )
        copy.start()

    def arrived(dst, recv_sem):
        pltpu.make_async_remote_copy(
            src_ref=dst,
            dst_ref=dst,
            send_sem=load_sem.at[0],
            recv_sem=recv_sem,
            device_id=partner,
            device_id_type=MESH,
        ).wait_recv()

    def left(src, send_sem):
        pltpu.make_async_remote_copy(
            src_ref=src,
            dst_ref=src,
            send_sem=send_sem,
            recv_sem=load_sem.at[0],
            device_id=partner,
            device_id_type=MESH,
        ).wait_send()

    small = [
        pltpu.make_async_copy(src, dst, small_sem.at[i])
        for i, (src, dst) in enumerate(
            [
                (lengths_hbm, lengths_ref),
                (queries_hbm, queries_ref),
                (expert_slot_hbm, expert_slot_ref),
                (gain_hbm, gain_ref),
                (router_hbm, router_ref),
                (routes_hbm, routes_ref),
                (residual_hbm, residual_ref),
            ]
        )
    ]

    loads = [
        pltpu.make_async_copy(src, dst, load_sem.at[min(i, 3)])
        for i, (src, dst) in enumerate(
            [
                (value_up_hbm, value_up),
                (out_proj_hbm, out_proj),
                (gate_up_hbm, gate_up),
            ]
            + [
                (down_hbm.at[e], down.at[:, pl.ds(e * down_hbm.shape[2], down_hbm.shape[2])])
                for e in range(local_experts)
            ]
        )
    ]
    cached = [
        pltpu.make_async_copy(cache_hbm.at[n], cache.at[n], cache_sem) for n in range(seqs)
    ]
    for load in small[:2] + cached + loads[:1]:
        load.start()

    barrier = pltpu.get_barrier_semaphore()
    peers = [partner] + [to_y(d) for d in ys] + [to_z(d) for d in zs] + [to_x(d) for d in xs]
    for device in peers:
        pl.semaphore_signal(barrier, inc=1, device_id=device, device_id_type=MESH)

    score_scale = (VHEAD + ROPE) ** (-0.5)
    for load in small[:2] + [pltpu.make_async_copy(cache_hbm, cache, cache_sem)]:
        load.wait()
    scores = []
    positions = lax.broadcasted_iota(jnp.int32, (head_count, cache.shape[2]), 1)
    for n in range(seqs):
        of_seq = dot(queries_ref[n], cache[n]) * score_scale
        scores.append(jnp.where(positions < lengths_ref[n], of_seq, -1e30))
    for load in small[2:] + loads[1:]:
        load.start()
    scores = jnp.concatenate(scores)
    exps = jnp.exp(scores - jnp.max(scores, axis=1, keepdims=True))
    probs = exps / jnp.sum(exps, axis=1, keepdims=True)
    for n in range(seqs):
        of_heads = slice(n * head_count, (n + 1) * head_count)
        of_seq = dot_nt(probs[of_heads].astype(BF16), cache[n, :latent_dim, :])
        for q in range(latent_dim // LANES):
            latent[q, of_heads, :] = of_seq[:, q * LANES : (q + 1) * LANES]
    loads[0].wait()
    half = head_count // 2
    for low in range(half):
        pair = []
        for h in (low, low + half):
            of_head = jnp.concatenate(
                [
                    latent[q, pl.ds(h, seqs, stride=head_count), :]
                    for q in range(latent_dim // LANES)
                ],
                axis=1,
            )
            pair.append(dot(of_head.astype(BF16), value_up[h]))
        heads[y, c, :, low * VHEAD : (low + 1) * VHEAD] = jnp.concatenate(pair, axis=0).astype(
            BF16
        )

    pl.semaphore_wait(barrier, len(peers))

    mine = heads.at[y, c]
    for d in far_ys:
        send(mine, mine, head_send, head_recv.at[d], to_y(d))
    send(mine, mine, head_core_send, head_core_recv, partner)

    for load in small[2:]:
        load.wait()
    gain_row = gain_ref[...].astype(F32)[None, :]
    router_all[c, g] = jnp.zeros(router_all.shape[2:], F32)
    router_all[c, g, :local_experts, :cols] = router_ref[...].astype(F32) * gain_row
    for d in xs:
        send(
            router_all.at[c, g], router_all.at[c, g], router_send.at[1], router_recv.at[1], to_x(d)
        )
    identity = (
        lax.broadcasted_iota(jnp.int32, (cols, cols), 0)
        == lax.broadcasted_iota(jnp.int32, (cols, cols), 1)
    ).astype(F32)
    gain_column = dot_nt(
        identity.astype(BF16), jnp.broadcast_to(gain_row, (LANES, cols)).astype(BF16)
    )
    loads[2].wait()
    for dst, first in ((weights_out, other * 2), (weights.at[c], c * 2)):
        dst[cols:, :] = jnp.zeros((wide_cols - cols, dst.shape[1]), BF16)
        for j in range(2):
            wide[...] = gate_up[first + j].astype(F32)
            for i in range(2):
                part = wide[pl.ds(i, cols, stride=2), :] * gain_column
                start = (2 * j + i) * LANES
                dst[:cols, start : start + LANES] = part.astype(BF16)
        if dst is weights_out:
            send(weights_out, weights.at[c], weight_send, weight_recv, partner)

    lane = lax.broadcasted_iota(jnp.int32, (block, LANES), 1)
    routes = routes_ref[...]
    slot_of = jnp.zeros(routes.shape, jnp.int32)
    for e in range(expert_slot_ref.shape[0]):
        slot_of = jnp.where(routes == e, expert_slot_ref[e], slot_of)
    used = cols - (wide_cols - LANES)
    slots = expert_slot_ref.shape[0]
    by_slot = jnp.zeros((slots, block), F32)
    slot_at = lax.broadcasted_iota(jnp.int32, (slots, block), 0)
    for k in range(routes.shape[0]):
        by_slot = by_slot + (slot_at == slot_of[k : k + 1, :]).astype(F32)
    same = lax.broadcasted_iota(jnp.int32, (block, block), 0) == lax.broadcasted_iota(
        jnp.int32, (block, block), 1
    )
    by_token = dot_nt(same.astype(F32), by_slot)
    place = lax.broadcasted_iota(jnp.int32, (slots, LANES), 1) - used
    place = (place == lax.broadcasted_iota(jnp.int32, (slots, LANES), 0)).astype(F32)
    extra[...] = dot(by_token, place)
    residual[:, wide_cols - LANES :] = jnp.zeros((block, LANES), F32)
    residual[:, :cols] = residual_ref[...].astype(F32)
    proj_out[:, :, wide_cols - LANES :] = jnp.zeros((nz, block, LANES), BF16)

    for d in ys:
        came = heads.at[at_y(-d), c]
        arrived(came, head_recv.at[d])
        send(came, came, head_core_send, head_core_recv, partner)
    loads[1].wait()
    arrived(heads.at[:, other], head_core_recv)

    gathered = heads[...].reshape(ny * 2 * 2 * seqs, half * VHEAD)
    low_part = dot_nt(gathered, out_proj[:, : half * VHEAD]).reshape(ny * 2, 2, seqs, cols)
    high_part = dot_nt(gathered, out_proj[:, half * VHEAD :]).reshape(ny * 2, 2, seqs, cols)
    attn = (low_part[:, 0] + high_part[:, 1]).reshape(nz, block, cols)
    proj_out[:, :, :cols] = attn.astype(BF16)
    for d in far_zs:
        send(proj_out.at[at_z(d)], proj_in.at[t], proj_send, proj_recv, to_z(d))

    arrived(router_all.at[c, pl.ds(1, nx - 1)], router_recv.at[1])
    send(router_all.at[c], router_all.at[c], router_send.at[0], router_recv.at[0], partner)
    arrived(weights.at[other], weight_recv)
    arrived(router_all.at[other], router_recv.at[0])
    pad = router_all.shape[2]
    slot_row = lax.broadcasted_iota(jnp.int32, (slots, nx * pad), 0)
    select = (
        lax.broadcasted_iota(jnp.int32, (slots, nx * pad), 1)
        == (slot_row // local_experts) * pad + lax.rem(slot_row, local_experts)
    ).astype(F32).astype(BF16)
    column = lax.broadcasted_iota(jnp.int32, (slots, wide_cols), 1)
    squares_at = (column == cols + slots) | (column == cols + slots + 1)
    for core in range(2):
        packed = router_all[core].reshape(nx * pad, wide_cols).astype(BF16)
        router_rows[core, :slots] = dot(select, packed).astype(BF16)
        router_rows[core, slots:] = squares_at.astype(F32).astype(BF16)

    total = residual[...] + proj_out[t].astype(F32)
    arrived(proj_in.at[pl.ds(1, nz - 1)], proj_recv)
    for d in zs:
        total = total + proj_in[at_z(-d)].astype(F32)
    total = total.astype(BF16).astype(F32)
    stream[...] = total
    squares = jnp.sum(total * total, axis=1, keepdims=True)
    upper = squares.astype(BF16).astype(F32)
    marks = extra[...]
    marks = jnp.where(lane == used + slots, upper, marks)
    marks = jnp.where(lane == used + slots + 1, squares - upper, marks)
    rows[c, g, t, :, : wide_cols - LANES] = total[:, : wide_cols - LANES].astype(BF16)
    rows[c, g, t, :, wide_cols - LANES :] = (total[:, wide_cols - LANES :] + marks).astype(BF16)

    mine = rows.at[c, g, t]
    for d in zs:
        send(mine, mine, row_z_send, row_z_recv.at[d], to_z(d))
    for a in (2, 1, 3):
        send(mine, mine, row_x_send.at[a], row_x_recv.at[a], to_x(a))
    for d in zs:
        came = rows.at[c, g, at_z(-d)]
        arrived(came, row_z_recv.at[d])
        for a in (2, 1, 3):
            send(came, came, row_x_send.at[a], row_x_recv.at[a], to_x(a))
    def pass_rows(a):
        came = rows.at[c, at_x(a)]
        if a:
            arrived(came, row_x_recv.at[a])
        send(came, came, row_core_send, row_core_recv.at[a], partner)

    def multiply_rows(a):
        of = at_x(a)
        part = dot(rows[c, of].reshape(nz * block, wide_cols), weights[c])
        arrived(rows.at[other, of], row_core_recv.at[a])
        part = part + dot(rows[other, of].reshape(nz * block, wide_cols), weights[other])
        part_out[of] = part.astype(BF16).reshape(nz, block, part.shape[1])
        of_half, place = [(0, 0), (1, 0), (0, 1), (1, 1)][a]
        for d in far_ys:
            send(
                part_out.at[of, at_y(d)],
                part_in.at[of_half, y, place],
                part_send,
                part_recv.at[of_half],
                to_y(d),
            )

    chunk = 2 * block
    halves = ((0, 2), (1, 3))
    per_tile = LANES // chunk

    def send_tail(h):
        missing = max(LANES - nz * chunk, 0)
        tail = jnp.zeros((2 * slots, nz * chunk + missing), F32)
        for core in range(2):
            by_owner = jnp.concatenate(
                [
                    rows[core, at_x(code)].reshape(nz, 1, block, wide_cols)
                    for code in halves[h]
                ],
                axis=1,
            ).reshape(nz * chunk, wide_cols)
            if missing:
                by_owner = jnp.concatenate([by_owner, jnp.zeros((missing, wide_cols), BF16)])
            tail = tail + dot_nt(router_rows[core], by_owner)
        lane_of = lax.broadcasted_iota(jnp.int32, (slots, LANES), 1)
        for q in range(ny):
            tile = slice(q // per_tile * LANES, (q // per_tile + 1) * LANES)
            turn = LANES - q % per_tile * chunk
            logits = pltpu.roll(tail[:slots, tile], turn % LANES, 1)
            sums = pltpu.roll(tail[slots:, tile], (turn + chunk) % LANES, 1)
            tail_out[h, q] = jnp.where(lane_of < chunk, logits, sums).astype(BF16)
        for d in far_ys:
            send(
                tail_out.at[h, at_y(d)],
                tail_in.at[h, y],
                tail_send,
                tail_recv.at[h],
                to_y(d),
            )

    pass_rows(0)
    multiply_rows(0)
    pass_rows(2)
    pass_rows(1)
    multiply_rows(2)
    send_tail(0)
    pass_rows(3)
    multiply_rows(1)
    multiply_rows(3)
    send_tail(1)

    down_at = lax.broadcasted_iota(jnp.int32, (chunk, LANES), 0)
    across = lax.broadcasted_iota(jnp.int32, (chunk, LANES), 1)
    slot_at = lax.broadcasted_iota(jnp.int32, (chunk, slots), 1)

    def find_hidden(h):
        tail = tail_out[h, y].astype(F32)
        total = jnp.concatenate([part_out[at_x(code), y] for code in halves[h]]).astype(F32)
        arrived(tail_in.at[h, pl.ds(1, ny - 1)], tail_recv.at[h])
        for d in ys:
            of = at_y(-d)
            tail = tail + tail_in[h, of].astype(F32)
        arrived(part_in.at[h, pl.ds(1, ny - 1)], part_recv.at[h])
        for d in ys:
            of = at_y(-d)
            total = total + part_in[h, of].reshape(total.shape).astype(F32)
        logits = dot_nt((across == down_at).astype(F32), tail, lax.Precision.HIGHEST)
        sums = dot_nt((across == down_at + chunk).astype(F32), tail, lax.Precision.HIGHEST)
        inv_rms = lax.rsqrt(sums / width + EPSILON)
        marks = jnp.concatenate(
            [rows[c, at_x(code), y, :, wide_cols - LANES :] for code in halves[h]]
        ).astype(F32)
        marks = pltpu.roll(marks, LANES - used, 1)[:, :slots]
        scores = jax.nn.sigmoid(logits * inv_rms) * marks
        shares = scores / jnp.sum(scores, axis=1, keepdims=True)
        inv_rms = inv_rms[:, :1]
        for j in range(2):
            chosen = slot_at == g * local_experts + c * 2 + j
            share = jnp.sum(jnp.where(chosen, shares, 0.0), axis=1, keepdims=True)
            gate = total[:, 2 * j * LANES : (2 * j + 1) * LANES] * inv_rms
            up = total[:, (2 * j + 1) * LANES : (2 * j + 2) * LANES] * inv_rms
            value = jax.nn.silu(gate) * up * share
            hidden[h, c, y, :, j * LANES : (j + 1) * LANES] = value.astype(BF16)
        mine = hidden.at[h, c, y]
        for d in ys:
            send(mine, mine, hid_send, hid_recv.at[h, d], to_y(d))
        send(mine, mine, hid_core_send, hid_core_recv.at[group_of(h, 0)], partner)

    down_out[:, :, :, :, wide_cols - LANES :] = jnp.zeros(down_out.shape[:4] + (LANES,), BF16)
    order = [0] + ys
    first = [order[i : i + 4] for i in range(0, ny, 4)]
    second = [order[i : i + 2] for i in range(0, ny, 2)]
    steps = [(0, group) for group in first] + [(1, group) for group in second]

    def group_of(h, d):
        return [half == h and d in group for half, group in steps].index(True)

    find_hidden(0)
    find_hidden(1)
    pltpu.make_async_copy(down, down, load_sem.at[3]).wait()
    split = down.shape[1] // 2

    def pass_hidden(h, d):
        if d:
            came = hidden.at[h, c, at_y(-d)]
            arrived(came, hid_recv.at[h, d])
            send(came, came, hid_core_send, hid_core_recv.at[group_of(h, d)], partner)

    def multiply_hidden(h, group):
        arrived(hidden.at[h, other, pl.ds(0, len(group))], hid_core_recv.at[group_of(h, group[0])])
        low_part = jnp.concatenate([hidden[h, 0, at_y(-d)] for d in group])
        high_part = jnp.concatenate([hidden[h, 1, at_y(-d)] for d in group])
        part = dot_nt(low_part, down[:, :split]) + dot_nt(high_part, down[:, split:])
        part = part.astype(BF16).reshape(len(group), 2, block, cols)
        for i, d in enumerate(group):
            of = at_y(-d)
            down_out[h, of, :, :, :cols] = part[i]
            for place, code in enumerate(halves[h]):
                if code:
                    send(
                        down_out.at[h, of, place],
                        down_in.at[code, of],
                        down_send,
                        down_recv.at[group_of(1, d) - len(first)],
                        to_x(code),
                    )

    def add_groups(group):
        here = down_in.at[pl.ds(1, nx - 1), pl.ds(0, len(group))]
        arrived(here, down_recv.at[second.index(group)])
        for d in group:
            of = at_y(-d)
            total = down_out[0, of, 0].astype(F32)
            for a in xs:
                total = total + down_in[a, of].astype(F32)
            sum_out[of] = total.astype(BF16)

            @pl.when(of != t)
            def _():
                send(sum_out.at[of], sum_in.at[t], sum_send, sum_recv, (g, dp, of))

    for d in steps[0][1]:
        pass_hidden(0, d)
    for i, (h, group) in enumerate(steps):
        if i + 1 < len(steps):
            for d in steps[i + 1][1]:
                pass_hidden(steps[i + 1][0], d)
        multiply_hidden(h, group)
        if i - len(first) >= 2:
            add_groups(second[i - len(first) - 2])
    for group in second[-2:]:
        add_groups(group)
    total = stream[...] + sum_out[t].astype(F32)
    arrived(sum_in.at[pl.ds(1, nz - 1)], sum_recv)
    for d in zs:
        of = at_z(-d)
        total = total + sum_in[of].astype(F32)
    out_ref[...] = total[:, :cols].astype(BF16)

    left(heads.at[pl.ds(1, ny - 1), c], head_send)
    left(heads.at[:, c], head_core_send)
    left(weights_out, weight_send)
    left(router_all.at[c, pl.ds(1, nx - 1)], router_send.at[1])
    left(router_all.at[c], router_send.at[0])
    left(proj_out.at[pl.ds(1, nz - 1)], proj_send)
    left(rows.at[c, g, pl.ds(1, nz - 1)], row_z_send)
    for a in xs:
        left(rows.at[c, g], row_x_send.at[a])
    left(rows.at[c], row_core_send)
    left(part_out.at[:, pl.ds(1, ny - 1)], part_send)
    left(tail_out.at[:, pl.ds(1, ny - 1)], tail_send)
    left(hidden.at[:, c, pl.ds(1, ny - 1)], hid_send)
    left(hidden.at[:, c], hid_core_send)
    left(down_in.at[pl.ds(1, nx - 1)], down_send)
    left(sum_out.at[pl.ds(1, nz - 1)], sum_send)


def on_device(sizes, width, *arrays):
    (
        queries,
        latent_cache,
        lengths,
        value_up,
        out_proj,
        residual_in,
        norm_gain,
        router,
        gate_up,
        down_proj,
        routes,
        expert_slot,
    ) = arrays
    nx, ny, nz = sizes
    seqs, head_count, depth = queries.shape
    block, cols = residual_in.shape
    experts, _, _, units = gate_up.shape
    gate_up = gate_up.reshape(experts, cols * 2, units)
    down_proj = jnp.swapaxes(down_proj, 1, 2)
    latent_cache = jnp.swapaxes(latent_cache, 1, 2)
    out_proj = out_proj.T
    routes = routes.T
    wide_cols = -(-cols // LANES) * LANES
    latent_dim = value_up.shape[1]
    slots = expert_slot.shape[0]
    vmem = pl.BlockSpec(memory_space=pltpu.VMEM)
    anywhere = pl.BlockSpec(memory_space=pltpu.HBM)
    sem = pltpu.SemaphoreType.DMA
    scratch = [
        pltpu.SMEM(lengths.shape, jnp.int32),
        pltpu.SMEM(expert_slot.shape, jnp.int32),
        pltpu.VMEM(queries.shape, BF16),
        pltpu.VMEM(residual_in.shape, BF16),
        pltpu.VMEM(norm_gain.shape, BF16),
        pltpu.VMEM(router.shape, BF16),
        pltpu.VMEM(routes.shape, jnp.int32),
        pltpu.VMEM(latent_cache.shape, BF16),
        pltpu.VMEM(value_up.shape, BF16),
        pltpu.VMEM(out_proj.shape, BF16),
        pltpu.VMEM(gate_up.shape, BF16),
        pltpu.VMEM((cols, experts * units), BF16),
        pltpu.VMEM((latent_dim // LANES, seqs * head_count, LANES), F32),
        pltpu.VMEM((ny, 2, 2 * seqs, head_count // 2 * VHEAD), BF16),
        pltpu.VMEM((nz, block, wide_cols), BF16),
        pltpu.VMEM((nz, block, wide_cols), BF16),
        pltpu.VMEM((block, wide_cols), F32),
        pltpu.VMEM((block, LANES), F32),
        pltpu.VMEM((block, wide_cols), F32),
        pltpu.VMEM((2, nx, nz, block, wide_cols), BF16),
        pltpu.VMEM((cols * 2, units), F32),
        pltpu.VMEM((2, wide_cols, 4 * units), BF16),
        pltpu.VMEM((wide_cols, 4 * units), BF16),
        pltpu.VMEM((2, nx, 8, wide_cols), F32),
        pltpu.VMEM((2, 2 * slots, wide_cols), BF16),
        pltpu.VMEM((nx, nz, block, 4 * units), BF16),
        pltpu.VMEM((2, ny, 2, block, 4 * units), BF16),
        pltpu.VMEM((2, ny, slots, LANES), BF16),
        pltpu.VMEM((2, ny, slots, LANES), BF16),
        pltpu.VMEM((2, 2, ny, 2 * block, 2 * units), BF16),
        pltpu.VMEM((2, ny, 2, block, wide_cols), BF16),
        pltpu.VMEM((nx, ny, block, wide_cols), BF16),
        pltpu.VMEM((nz, block, wide_cols), BF16),
        pltpu.VMEM((nz, block, wide_cols), BF16),
        sem((4,)),
        sem,
        sem((7,)),
        sem,
        sem((ny,)),
        sem,
        sem,
        sem,
        sem,
        sem((2,)),
        sem((2,)),
        sem,
        sem,
        sem,
        sem((nz,)),
        sem((nx,)),
        sem((nx,)),
        sem,
        sem((nx,)),
        sem,
        sem((2,)),
        sem,
        sem((2,)),
        sem,
        sem((2, ny)),
        sem,
        sem((ny,)),
        sem,
        sem((ny,)),
        sem,
        sem,
    ]
    return pl.pallas_call(
        functools.partial(kernel, sizes, width),
        out_shape=pltpu.VMEM((block, cols), BF16),
        in_specs=[anywhere] * 12,
        out_specs=vmem,
        scratch_shapes=scratch,
        name="decode_layer",
        compiler_params=pltpu.CompilerParams(
            collective_id=0, has_side_effects=True, vmem_limit_bytes=60 * 2**20
        ),
    )(
        lengths,
        expert_slot,
        queries,
        residual_in,
        norm_gain,
        router,
        routes,
        latent_cache,
        value_up,
        out_proj,
        gate_up,
        down_proj,
    )


def solution(mesh):
    in_specs = (
        P(("grp", "dp"), "tensor", None),
        P(("grp", "dp"), None, None),
        P(("grp", "dp")),
        P("tensor", None, None),
        P("tensor", "dp"),
        P(("grp", "tensor"), "dp"),
        P("dp"),
        P("grp", "dp"),
        P("grp", "dp", None, "tensor"),
        P("grp", "tensor", "dp"),
        P(("grp", "tensor"), None),
        P(),
    )
    out_specs = P(("grp", "tensor"), "dp")
    sizes = (mesh.shape["grp"], mesh.shape["dp"] // 2, mesh.shape["tensor"])

    def whole(*arrays):
        width = arrays[5].shape[1]
        return jax.shard_map(
            functools.partial(on_device, sizes, width),
            mesh=mesh,
            in_specs=in_specs,
            out_specs=out_specs,
            check_vma=False,
        )(*arrays)

    return whole
```

```python
import functools

import jax
import jax.numpy as jnp
from jax import lax
from jax.experimental import pallas as pl
from jax.experimental.pallas import tpu as pltpu
from jax.sharding import PartitionSpec as P

ROPE = 64
VHEAD = 128
EPSILON = 1e-06
MESH = pl.DeviceIdType.MESH
BF16 = jnp.bfloat16
F32 = jnp.float32
LANES = 128


def dot(a, b):
    return jnp.dot(a, b, preferred_element_type=F32)


def dot_nt(a, b, precision=None):
    return lax.dot_general(
        a, b, (((1,), (1,)), ((), ())), preferred_element_type=F32, precision=precision
    )


def near_first(count):
    return sorted(range(1, count), key=lambda d: (min(d, count - d), d))


def kernel(
    sizes,
    width,
    lengths_hbm,
    expert_slot_hbm,
    queries_hbm,
    residual_hbm,
    gain_hbm,
    router_hbm,
    routes_hbm,
    cache_hbm,
    value_up_hbm,
    out_proj_hbm,
    gate_up_hbm,
    down_hbm,
    out_ref,
    lengths_ref,
    expert_slot_ref,
    queries_ref,
    residual_ref,
    gain_ref,
    router_ref,
    routes_ref,
    cache,
    value_up,
    out_proj,
    gate_up,
    down,
    latent,
    heads,
    proj_out,
    proj_in,
    residual,
    extra,
    stream,
    rows,
    wide,
    weights,
    weights_out,
    router_all,
    router_rows,
    part_out,
    part_in,
    tail_out,
    tail_in,
    hidden,
    down_out,
    down_in,
    sum_out,
    sum_in,
    load_sem,
    cache_sem,
    small_sem,
    head_send,
    head_recv,
    head_core_send,
    head_core_recv,
    weight_send,
    weight_recv,
    router_send,
    router_recv,
    proj_send,
    proj_recv,
    row_z_send,
    row_z_recv,
    row_x_send,
    row_x_recv,
    row_core_send,
    row_core_recv,
    part_send,
    part_recv,
    tail_send,
    tail_recv,
    hid_send,
    hid_recv,
    hid_core_send,
    hid_core_recv,
    down_send,
    down_recv,
    sum_send,
    sum_recv,
):
    nx, ny, nz = sizes
    g = lax.axis_index("grp")
    dp = lax.axis_index("dp")
    t = lax.axis_index("tensor")
    y = dp // 2
    c = lax.rem(dp, 2)
    other = 1 - c
    cols = residual_ref.shape[1]
    block = residual_ref.shape[0]
    wide_cols = stream.shape[1]
    seqs, head_count, depth = queries_ref.shape
    latent_dim = value_up.shape[1]
    local_experts = router_ref.shape[0]
    ys, zs = near_first(ny), near_first(nz)
    xs = [1, 3, 2]
    far_ys, far_zs = ys[::-1], zs[::-1]

    def at_x(code):
        return [g, g + 1 - 2 * lax.rem(g, 2), lax.rem(g + 2, nx), nx - 1 - g][code]

    def at_y(d):
        return lax.rem(y + ny + d, ny)

    def at_z(d):
        return lax.rem(t + nz + d, nz)

    def to_x(d):
        return (at_x(d), dp, t)

    def to_y(d):
        return (g, at_y(d) * 2 + c, t)

    def to_z(d):
        return (g, dp, at_z(d))

    partner = (g, y * 2 + other, t)

    def send(src, dst, send_sem, recv_sem, device):
        copy = pltpu.make_async_remote_copy(
            src_ref=src,
            dst_ref=dst,
            send_sem=send_sem,
            recv_sem=recv_sem,
            device_id=device,
            device_id_type=MESH,
        )
        copy.start()

    def arrived(dst, recv_sem):
        pltpu.make_async_remote_copy(
            src_ref=dst,
            dst_ref=dst,
            send_sem=load_sem.at[0],
            recv_sem=recv_sem,
            device_id=partner,
            device_id_type=MESH,
        ).wait_recv()

    def left(src, send_sem):
        pltpu.make_async_remote_copy(
            src_ref=src,
            dst_ref=src,
            send_sem=send_sem,
            recv_sem=load_sem.at[0],
            device_id=partner,
            device_id_type=MESH,
        ).wait_send()

    small = [
        pltpu.make_async_copy(src, dst, small_sem.at[i])
        for i, (src, dst) in enumerate(
            [
                (lengths_hbm, lengths_ref),
                (queries_hbm, queries_ref),
                (expert_slot_hbm, expert_slot_ref),
                (gain_hbm, gain_ref),
                (router_hbm, router_ref),
                (routes_hbm, routes_ref),
                (residual_hbm, residual_ref),
            ]
        )
    ]

    loads = [
        pltpu.make_async_copy(src, dst, load_sem.at[min(i, 3)])
        for i, (src, dst) in enumerate(
            [
                (value_up_hbm, value_up),
                (out_proj_hbm, out_proj),
                (gate_up_hbm, gate_up),
            ]
            + [
                (down_hbm.at[e], down.at[:, pl.ds(e * down_hbm.shape[2], down_hbm.shape[2])])
                for e in range(local_experts)
            ]
        )
    ]
    cached = [
        pltpu.make_async_copy(cache_hbm.at[n], cache.at[n], cache_sem) for n in range(seqs)
    ]
    for load in small[:2] + cached + loads[:1]:
        load.start()

    barrier = pltpu.get_barrier_semaphore()
    peers = [to_y(d) for d in far_ys] + [to_z(d) for d in far_zs] + [to_x(d) for d in xs] + [partner]
    for device in peers:
        pl.semaphore_signal(barrier, inc=1, device_id=device, device_id_type=MESH)

    score_scale = (VHEAD + ROPE) ** (-0.5)
    for load in small[:2] + [pltpu.make_async_copy(cache_hbm, cache, cache_sem)]:
        load.wait()
    scores = []
    positions = lax.broadcasted_iota(jnp.int32, (head_count, cache.shape[2]), 1)
    for n in range(seqs):
        of_seq = dot(queries_ref[n], cache[n]) * score_scale
        scores.append(jnp.where(positions < lengths_ref[n], of_seq, -1e30))
    for load in small[2:] + loads[1:]:
        load.start()
    scores = jnp.concatenate(scores)
    exps = jnp.exp(scores - jnp.max(scores, axis=1, keepdims=True))
    probs = exps / jnp.sum(exps, axis=1, keepdims=True)
    for n in range(seqs):
        of_heads = slice(n * head_count, (n + 1) * head_count)
        of_seq = dot_nt(probs[of_heads].astype(BF16), cache[n, :latent_dim, :])
        for q in range(latent_dim // LANES):
            latent[q, of_heads, :] = of_seq[:, q * LANES : (q + 1) * LANES]
    loads[0].wait()
    half = head_count // 2
    for low in range(half):
        pair = []
        for h in (low, low + half):
            of_head = jnp.concatenate(
                [
                    latent[q, pl.ds(h, seqs, stride=head_count), :]
                    for q in range(latent_dim // LANES)
                ],
                axis=1,
            )
            pair.append(dot(of_head.astype(BF16), value_up[h]))
        heads[y, c, :, low * VHEAD : (low + 1) * VHEAD] = jnp.concatenate(pair, axis=0).astype(
            BF16
        )

    pl.semaphore_wait(barrier, len(peers))

    mine = heads.at[y, c]
    for d in far_ys:
        send(mine, mine, head_send, head_recv.at[d], to_y(d))
    send(mine, mine, head_core_send, head_core_recv, partner)

    for load in small[2:]:
        load.wait()
    gain_row = gain_ref[...].astype(F32)[None, :]
    router_all[c, g] = jnp.zeros(router_all.shape[2:], F32)
    router_all[c, g, :local_experts, :cols] = router_ref[...].astype(F32) * gain_row
    for d in xs:
        send(
            router_all.at[c, g], router_all.at[c, g], router_send.at[1], router_recv.at[1], to_x(d)
        )
    identity = (
        lax.broadcasted_iota(jnp.int32, (cols, cols), 0)
        == lax.broadcasted_iota(jnp.int32, (cols, cols), 1)
    ).astype(F32)
    gain_column = dot_nt(
        identity.astype(BF16), jnp.broadcast_to(gain_row, (LANES, cols)).astype(BF16)
    )
    loads[2].wait()
    for dst, first in ((weights_out, other * 2), (weights.at[c], c * 2)):
        dst[cols:, :] = jnp.zeros((wide_cols - cols, dst.shape[1]), BF16)
        for j in range(2):
            wide[...] = gate_up[first + j].astype(F32)
            for i in range(2):
                part = wide[pl.ds(i, cols, stride=2), :] * gain_column
                start = (2 * j + i) * LANES
                dst[:cols, start : start + LANES] = part.astype(BF16)
        if dst is weights_out:
            send(weights_out, weights.at[c], weight_send, weight_recv, partner)

    lane = lax.broadcasted_iota(jnp.int32, (block, LANES), 1)
    routes = routes_ref[...]
    slot_of = jnp.zeros(routes.shape, jnp.int32)
    for e in range(expert_slot_ref.shape[0]):
        slot_of = jnp.where(routes == e, expert_slot_ref[e], slot_of)
    used = cols - (wide_cols - LANES)
    slots = expert_slot_ref.shape[0]
    by_slot = jnp.zeros((slots, block), F32)
    slot_at = lax.broadcasted_iota(jnp.int32, (slots, block), 0)
    for k in range(routes.shape[0]):
        by_slot = by_slot + (slot_at == slot_of[k : k + 1, :]).astype(F32)
    same = lax.broadcasted_iota(jnp.int32, (block, block), 0) == lax.broadcasted_iota(
        jnp.int32, (block, block), 1
    )
    by_token = dot_nt(same.astype(F32), by_slot)
    place = lax.broadcasted_iota(jnp.int32, (slots, LANES), 1) - used
    place = (place == lax.broadcasted_iota(jnp.int32, (slots, LANES), 0)).astype(F32)
    extra[...] = dot(by_token, place)
    residual[:, wide_cols - LANES :] = jnp.zeros((block, LANES), F32)
    residual[:, :cols] = residual_ref[...].astype(F32)
    proj_out[:, :, wide_cols - LANES :] = jnp.zeros((nz, block, LANES), BF16)

    for d in ys:
        came = heads.at[at_y(-d), c]
        arrived(came, head_recv.at[d])
        send(came, came, head_core_send, head_core_recv, partner)
    loads[1].wait()
    arrived(heads.at[:, other], head_core_recv)

    gathered = heads[...].reshape(ny * 2 * 2 * seqs, half * VHEAD)
    low_part = dot_nt(gathered, out_proj[:, : half * VHEAD]).reshape(ny * 2, 2, seqs, cols)
    high_part = dot_nt(gathered, out_proj[:, half * VHEAD :]).reshape(ny * 2, 2, seqs, cols)
    attn = (low_part[:, 0] + high_part[:, 1]).reshape(nz, block, cols)
    proj_out[:, :, :cols] = attn.astype(BF16)
    for d in far_zs:
        send(proj_out.at[at_z(d)], proj_in.at[t], proj_send, proj_recv, to_z(d))

    arrived(router_all.at[c, pl.ds(1, nx - 1)], router_recv.at[1])
    send(router_all.at[c], router_all.at[c], router_send.at[0], router_recv.at[0], partner)
    arrived(weights.at[other], weight_recv)
    arrived(router_all.at[other], router_recv.at[0])
    pad = router_all.shape[2]
    slot_row = lax.broadcasted_iota(jnp.int32, (slots, nx * pad), 0)
    select = (
        lax.broadcasted_iota(jnp.int32, (slots, nx * pad), 1)
        == (slot_row // local_experts) * pad + lax.rem(slot_row, local_experts)
    ).astype(F32).astype(BF16)
    column = lax.broadcasted_iota(jnp.int32, (slots, wide_cols), 1)
    squares_at = (column == cols + slots) | (column == cols + slots + 1)
    for core in range(2):
        packed = router_all[core].reshape(nx * pad, wide_cols).astype(BF16)
        router_rows[core, :slots] = dot(select, packed).astype(BF16)
        router_rows[core, slots:] = squares_at.astype(F32).astype(BF16)

    total = residual[...] + proj_out[t].astype(F32)
    arrived(proj_in.at[pl.ds(1, nz - 1)], proj_recv)
    for d in zs:
        total = total + proj_in[at_z(-d)].astype(F32)
    total = total.astype(BF16).astype(F32)
    stream[...] = total
    squares = jnp.sum(total * total, axis=1, keepdims=True)
    upper = squares.astype(BF16).astype(F32)
    marks = extra[...]
    marks = jnp.where(lane == used + slots, upper, marks)
    marks = jnp.where(lane == used + slots + 1, squares - upper, marks)
    rows[c, g, t, :, : wide_cols - LANES] = total[:, : wide_cols - LANES].astype(BF16)
    rows[c, g, t, :, wide_cols - LANES :] = (total[:, wide_cols - LANES :] + marks).astype(BF16)

    mine = rows.at[c, g, t]
    for d in zs:
        send(mine, mine, row_z_send, row_z_recv.at[d], to_z(d))
    for a in (2, 1, 3):
        send(mine, mine, row_x_send.at[a], row_x_recv.at[a], to_x(a))
    for d in zs:
        came = rows.at[c, g, at_z(-d)]
        arrived(came, row_z_recv.at[d])
        for a in (2, 1, 3):
            send(came, came, row_x_send.at[a], row_x_recv.at[a], to_x(a))
    def pass_rows(a):
        came = rows.at[c, at_x(a)]
        if a:
            arrived(came, row_x_recv.at[a])
        send(came, came, row_core_send, row_core_recv.at[a], partner)

    def multiply_rows(a):
        of = at_x(a)
        part = dot(rows[c, of].reshape(nz * block, wide_cols), weights[c])
        arrived(rows.at[other, of], row_core_recv.at[a])
        part = part + dot(rows[other, of].reshape(nz * block, wide_cols), weights[other])
        part_out[of] = part.astype(BF16).reshape(nz, block, part.shape[1])
        of_half, place = [(0, 0), (1, 0), (0, 1), (1, 1)][a]
        for d in far_ys:
            send(
                part_out.at[of, at_y(d)],
                part_in.at[of_half, y, place],
                part_send,
                part_recv.at[of_half],
                to_y(d),
            )

    chunk = 2 * block
    halves = ((0, 2), (1, 3))
    per_tile = LANES // chunk

    def send_tail(h):
        missing = max(LANES - nz * chunk, 0)
        tail = jnp.zeros((2 * slots, nz * chunk + missing), F32)
        for core in range(2):
            by_owner = jnp.concatenate(
                [
                    rows[core, at_x(code)].reshape(nz, 1, block, wide_cols)
                    for code in halves[h]
                ],
                axis=1,
            ).reshape(nz * chunk, wide_cols)
            if missing:
                by_owner = jnp.concatenate([by_owner, jnp.zeros((missing, wide_cols), BF16)])
            tail = tail + dot_nt(router_rows[core], by_owner)
        lane_of = lax.broadcasted_iota(jnp.int32, (slots, LANES), 1)
        for q in range(ny):
            tile = slice(q // per_tile * LANES, (q // per_tile + 1) * LANES)
            turn = LANES - q % per_tile * chunk
            logits = pltpu.roll(tail[:slots, tile], turn % LANES, 1)
            sums = pltpu.roll(tail[slots:, tile], (turn + chunk) % LANES, 1)
            tail_out[h, q] = jnp.where(lane_of < chunk, logits, sums).astype(BF16)
        for d in far_ys:
            send(
                tail_out.at[h, at_y(d)],
                tail_in.at[h, y],
                tail_send,
                tail_recv.at[h],
                to_y(d),
            )

    pass_rows(0)
    multiply_rows(0)
    pass_rows(2)
    pass_rows(1)
    multiply_rows(2)
    send_tail(0)
    pass_rows(3)
    multiply_rows(1)
    multiply_rows(3)
    send_tail(1)

    down_at = lax.broadcasted_iota(jnp.int32, (chunk, LANES), 0)
    across = lax.broadcasted_iota(jnp.int32, (chunk, LANES), 1)
    slot_at = lax.broadcasted_iota(jnp.int32, (chunk, slots), 1)

    def find_hidden(h):
        tail = tail_out[h, y].astype(F32)
        total = jnp.concatenate([part_out[at_x(code), y] for code in halves[h]]).astype(F32)
        arrived(tail_in.at[h, pl.ds(1, ny - 1)], tail_recv.at[h])
        for d in ys:
            of = at_y(-d)
            tail = tail + tail_in[h, of].astype(F32)
        arrived(part_in.at[h, pl.ds(1, ny - 1)], part_recv.at[h])
        for d in ys:
            of = at_y(-d)
            total = total + part_in[h, of].reshape(total.shape).astype(F32)
        logits = dot_nt((across == down_at).astype(F32), tail, lax.Precision.HIGHEST)
        sums = dot_nt((across == down_at + chunk).astype(F32), tail, lax.Precision.HIGHEST)
        inv_rms = lax.rsqrt(sums / width + EPSILON)
        marks = jnp.concatenate(
            [rows[c, at_x(code), y, :, wide_cols - LANES :] for code in halves[h]]
        ).astype(F32)
        marks = pltpu.roll(marks, LANES - used, 1)[:, :slots]
        scores = jax.nn.sigmoid(logits * inv_rms) * marks
        shares = scores / jnp.sum(scores, axis=1, keepdims=True)
        inv_rms = inv_rms[:, :1]
        for j in range(2):
            chosen = slot_at == g * local_experts + c * 2 + j
            share = jnp.sum(jnp.where(chosen, shares, 0.0), axis=1, keepdims=True)
            gate = total[:, 2 * j * LANES : (2 * j + 1) * LANES] * inv_rms
            up = total[:, (2 * j + 1) * LANES : (2 * j + 2) * LANES] * inv_rms
            value = jax.nn.silu(gate) * up * share
            hidden[h, c, y, :, j * LANES : (j + 1) * LANES] = value.astype(BF16)
        mine = hidden.at[h, c, y]
        for d in ys:
            send(mine, mine, hid_send, hid_recv.at[h, d], to_y(d))
        send(mine, mine, hid_core_send, hid_core_recv.at[group_of(h, 0)], partner)

    down_out[:, :, :, :, wide_cols - LANES :] = jnp.zeros(down_out.shape[:4] + (LANES,), BF16)
    order = [0] + ys
    first = [order[i : i + 4] for i in range(0, ny, 4)]
    second = [order[i : i + 2] for i in range(0, ny, 2)]
    steps = [(0, group) for group in first] + [(1, group) for group in second]

    def group_of(h, d):
        return [half == h and d in group for half, group in steps].index(True)

    find_hidden(0)
    find_hidden(1)
    pltpu.make_async_copy(down, down, load_sem.at[3]).wait()
    split = down.shape[1] // 2

    def pass_hidden(h, d):
        if d:
            came = hidden.at[h, c, at_y(-d)]
            arrived(came, hid_recv.at[h, d])
            send(came, came, hid_core_send, hid_core_recv.at[group_of(h, d)], partner)

    def multiply_hidden(h, group):
        arrived(hidden.at[h, other, pl.ds(0, len(group))], hid_core_recv.at[group_of(h, group[0])])
        low_part = jnp.concatenate([hidden[h, 0, at_y(-d)] for d in group])
        high_part = jnp.concatenate([hidden[h, 1, at_y(-d)] for d in group])
        part = dot_nt(low_part, down[:, :split]) + dot_nt(high_part, down[:, split:])
        part = part.astype(BF16).reshape(len(group), 2, block, cols)
        for i, d in enumerate(group):
            of = at_y(-d)
            down_out[h, of, :, :, :cols] = part[i]
            for place, code in enumerate(halves[h]):
                if code:
                    send(
                        down_out.at[h, of, place],
                        down_in.at[code, of],
                        down_send,
                        down_recv.at[group_of(1, d) - len(first)],
                        to_x(code),
                    )

    def add_groups(group):
        here = down_in.at[pl.ds(1, nx - 1), pl.ds(0, len(group))]
        arrived(here, down_recv.at[second.index(group)])
        for d in group:
            of = at_y(-d)
            total = down_out[0, of, 0].astype(F32)
            for a in xs:
                total = total + down_in[a, of].astype(F32)
            sum_out[of] = total.astype(BF16)

            @pl.when(of != t)
            def _():
                send(sum_out.at[of], sum_in.at[t], sum_send, sum_recv, (g, dp, of))

    for d in steps[0][1]:
        pass_hidden(0, d)
    for i, (h, group) in enumerate(steps):
        if i + 1 < len(steps):
            for d in steps[i + 1][1]:
                pass_hidden(steps[i + 1][0], d)
        multiply_hidden(h, group)
        if i - len(first) >= 2:
            add_groups(second[i - len(first) - 2])
    for group in second[-2:]:
        add_groups(group)
    total = stream[...] + sum_out[t].astype(F32)
    arrived(sum_in.at[pl.ds(1, nz - 1)], sum_recv)
    for d in zs:
        of = at_z(-d)
        total = total + sum_in[of].astype(F32)
    out_ref[...] = total[:, :cols].astype(BF16)

    left(heads.at[pl.ds(1, ny - 1), c], head_send)
    left(heads.at[:, c], head_core_send)
    left(weights_out, weight_send)
    left(router_all.at[c, pl.ds(1, nx - 1)], router_send.at[1])
    left(router_all.at[c], router_send.at[0])
    left(proj_out.at[pl.ds(1, nz - 1)], proj_send)
    left(rows.at[c, g, pl.ds(1, nz - 1)], row_z_send)
    for a in xs:
        left(rows.at[c, g], row_x_send.at[a])
    left(rows.at[c], row_core_send)
    left(part_out.at[:, pl.ds(1, ny - 1)], part_send)
    left(tail_out.at[:, pl.ds(1, ny - 1)], tail_send)
    left(hidden.at[:, c, pl.ds(1, ny - 1)], hid_send)
    left(hidden.at[:, c], hid_core_send)
    left(down_in.at[pl.ds(1, nx - 1)], down_send)
    left(sum_out.at[pl.ds(1, nz - 1)], sum_send)


def on_device(sizes, width, *arrays):
    (
        queries,
        latent_cache,
        lengths,
        value_up,
        out_proj,
        residual_in,
        norm_gain,
        router,
        gate_up,
        down_proj,
        routes,
        expert_slot,
    ) = arrays
    nx, ny, nz = sizes
    seqs, head_count, depth = queries.shape
    block, cols = residual_in.shape
    experts, _, _, units = gate_up.shape
    gate_up = gate_up.reshape(experts, cols * 2, units)
    down_proj = jnp.swapaxes(down_proj, 1, 2)
    latent_cache = jnp.swapaxes(latent_cache, 1, 2)
    out_proj = out_proj.T
    routes = routes.T
    wide_cols = -(-cols // LANES) * LANES
    latent_dim = value_up.shape[1]
    slots = expert_slot.shape[0]
    vmem = pl.BlockSpec(memory_space=pltpu.VMEM)
    anywhere = pl.BlockSpec(memory_space=pltpu.HBM)
    sem = pltpu.SemaphoreType.DMA
    scratch = [
        pltpu.SMEM(lengths.shape, jnp.int32),
        pltpu.SMEM(expert_slot.shape, jnp.int32),
        pltpu.VMEM(queries.shape, BF16),
        pltpu.VMEM(residual_in.shape, BF16),
        pltpu.VMEM(norm_gain.shape, BF16),
        pltpu.VMEM(router.shape, BF16),
        pltpu.VMEM(routes.shape, jnp.int32),
        pltpu.VMEM(latent_cache.shape, BF16),
        pltpu.VMEM(value_up.shape, BF16),
        pltpu.VMEM(out_proj.shape, BF16),
        pltpu.VMEM(gate_up.shape, BF16),
        pltpu.VMEM((cols, experts * units), BF16),
        pltpu.VMEM((latent_dim // LANES, seqs * head_count, LANES), F32),
        pltpu.VMEM((ny, 2, 2 * seqs, head_count // 2 * VHEAD), BF16),
        pltpu.VMEM((nz, block, wide_cols), BF16),
        pltpu.VMEM((nz, block, wide_cols), BF16),
        pltpu.VMEM((block, wide_cols), F32),
        pltpu.VMEM((block, LANES), F32),
        pltpu.VMEM((block, wide_cols), F32),
        pltpu.VMEM((2, nx, nz, block, wide_cols), BF16),
        pltpu.VMEM((cols * 2, units), F32),
        pltpu.VMEM((2, wide_cols, 4 * units), BF16),
        pltpu.VMEM((wide_cols, 4 * units), BF16),
        pltpu.VMEM((2, nx, 8, wide_cols), F32),
        pltpu.VMEM((2, 2 * slots, wide_cols), BF16),
        pltpu.VMEM((nx, nz, block, 4 * units), BF16),
        pltpu.VMEM((2, ny, 2, block, 4 * units), BF16),
        pltpu.VMEM((2, ny, slots, LANES), BF16),
        pltpu.VMEM((2, ny, slots, LANES), BF16),
        pltpu.VMEM((2, 2, ny, 2 * block, 2 * units), BF16),
        pltpu.VMEM((2, ny, 2, block, wide_cols), BF16),
        pltpu.VMEM((nx, ny, block, wide_cols), BF16),
        pltpu.VMEM((nz, block, wide_cols), BF16),
        pltpu.VMEM((nz, block, wide_cols), BF16),
        sem((4,)),
        sem,
        sem((7,)),
        sem,
        sem((ny,)),
        sem,
        sem,
        sem,
        sem,
        sem((2,)),
        sem((2,)),
        sem,
        sem,
        sem,
        sem((nz,)),
        sem((nx,)),
        sem((nx,)),
        sem,
        sem((nx,)),
        sem,
        sem((2,)),
        sem,
        sem((2,)),
        sem,
        sem((2, ny)),
        sem,
        sem((max(ny - 2, 4),)),
        sem,
        sem((max(ny // 2, 1),)),
        sem,
        sem,
    ]
    return pl.pallas_call(
        functools.partial(kernel, sizes, width),
        out_shape=pltpu.VMEM((block, cols), BF16),
        in_specs=[anywhere] * 12,
        out_specs=vmem,
        scratch_shapes=scratch,
        name="decode_layer",
        compiler_params=pltpu.CompilerParams(
            collective_id=0, has_side_effects=True, vmem_limit_bytes=60 * 2**20
        ),
    )(
        lengths,
        expert_slot,
        queries,
        residual_in,
        norm_gain,
        router,
        routes,
        latent_cache,
        value_up,
        out_proj,
        gate_up,
        down_proj,
    )


def solution(mesh):
    in_specs = (
        P(("grp", "dp"), "tensor", None),
        P(("grp", "dp"), None, None),
        P(("grp", "dp")),
        P("tensor", None, None),
        P("tensor", "dp"),
        P(("grp", "tensor"), "dp"),
        P("dp"),
        P("grp", "dp"),
        P("grp", "dp", None, "tensor"),
        P("grp", "tensor", "dp"),
        P(("grp", "tensor"), None),
        P(),
    )
    out_specs = P(("grp", "tensor"), "dp")
    sizes = (mesh.shape["grp"], mesh.shape["dp"] // 2, mesh.shape["tensor"])

    def whole(*arrays):
        width = arrays[5].shape[1]
        return jax.shard_map(
            functools.partial(on_device, sizes, width),
            mesh=mesh,
            in_specs=in_specs,
            out_specs=out_specs,
            check_vma=False,
        )(*arrays)

    return whole
```
